32 devices in a mesh: tm: 16 (over z, y, x), head: 2 (over core).
Axes of the slice: x: 2, y: 2, z: 4, core: 2. Of those that a mesh axis runs over, the one named last changes fastest.
Arguments:
- queries: bfloat16 [4096, 3072], P('tm', 'head'), may hold values from -6 to 6
- keys: bfloat16 [2048, 3072], P('tm', 'head'), may hold values from -6 to 6
- values: bfloat16 [2048, 3072], P('tm', 'head'), may hold values from -6 to 6
- out_weight: bfloat16 [3072, 3072], P('head'), may hold values from -0.109375 to 0.109375
- out_grad: bfloat16 [4096, 3072], P('tm', 'head'), may hold values from -6 to 6
- align_lists: int32 [16, 4], replicated, may hold values from -1 to 15, as said below
- block_masks: int32 [32, 3], P('tm'), may hold values from -1 to 3, as said below
Outputs:
- mixed: bfloat16 [4096, 3072], P('tm', 'head')
- query_grad: bfloat16 [4096, 3072], P('tm', 'head')
- key_grad: bfloat16 [2048, 3072], P('tm', 'head')
- value_grad: bfloat16 [2048, 3072], P('tm', 'head')
The draws below stay inside these ranges and needn't reach their ends.
Inputs may be any that keep to these rules, and one draw needn't show every extreme that they name: `align_lists`: row t holds a band of consecutive audio tile indices in its first slots and -1 in the rest; every listed tile a satisfies (t - 3) <= a < (t + 4). Some slab uses all 4 slots starting at (t - 3), and some slab's band ends at (t + 4) - 1. `block_masks`: row i names one or more consecutive used slots of the list of slab i // 2 in its first entries and -1 in the rest; some row has all 3 entries live.
All inputs are finite; a program needn't handle non-finite values.
Results may differ from the reference program's by a relative error of at most 0.025.
Values may be sent and summed in bfloat16 or wider, within the bound.
A program may use at most 128 MiB of HBM per device.

```python
import math
import jax
import jax.numpy as jnp
from jax import lax

D = 3072
HEADS = 24
HEAD_DIM = 128
TILE = 128
VT_DEV = 2
AB_DEV = 1
LIST = 4
BLOCKS = 3
REACH = 3
SLABS = 16
INNER = 3072
VTILES = 32
ATILES = 16
VIDEO = 4096
AUDIO = 2048
N_HEAD = 2


def draw_layout(key):
    base_key = jax.random.fold_in(key, 11)
    k_len, k_start, k_pick, k_count, k_shift = jax.random.split(base_key, 5)
    slab_index = jnp.arange(SLABS)
    region_lo = jnp.maximum(0, (slab_index - REACH) * AB_DEV)
    region_hi = jnp.minimum(ATILES, (slab_index + REACH + 1) * AB_DEV)
    band_len = jax.random.randint(k_len, (SLABS,), 1, LIST + 1)
    inner_span = SLABS - 2 * REACH
    full_slab = REACH + jax.random.randint(k_pick, (), 0, inner_span)
    edge_slab = REACH + (full_slab - REACH + 1) % inner_span
    band_len = jnp.where((slab_index == full_slab) | (slab_index == edge_slab), LIST, band_len)
    free_room = region_hi - region_lo - band_len + 1
    band_start = region_lo + jax.random.randint(k_start, (SLABS,), 0, 1 << 20) % free_room
    band_start = jnp.where(slab_index == full_slab, region_lo, band_start)
    band_start = jnp.where(slab_index == edge_slab, region_hi - band_len, band_start)
    slot_index = jnp.arange(LIST)
    align_table = jnp.where(slot_index[None, :] < band_len[:, None], band_start[:, None] + slot_index[None, :], -1)
    tile_slab = jnp.arange(VTILES) // VT_DEV
    tile_band = band_len[tile_slab]
    most_live = jnp.minimum(BLOCKS, tile_band)
    live_count = 1 + jax.random.randint(k_count, (VTILES,), 0, 1 << 20) % most_live
    live_count = jnp.where(jnp.arange(VTILES) == full_slab * VT_DEV, BLOCKS, live_count)
    live_offset = jax.random.randint(k_shift, (VTILES,), 0, 1 << 20) % (tile_band - live_count + 1)
    place_index = jnp.arange(BLOCKS)
    block_table = jnp.where(place_index[None, :] < live_count[:, None], live_offset[:, None] + place_index[None, :], -1)
    return (align_table.astype(jnp.int32), block_table.astype(jnp.int32))


def audio_keys(key):
    raw_keys = jax.random.normal(jax.random.fold_in(key, 23), (AUDIO, HEADS * HEAD_DIM), jnp.float32)
    raw_keys = jnp.clip(raw_keys, -6.0, 6.0)
    return raw_keys


def draw_align_lists(key, part):
    return draw_layout(key)[0]


def draw_block_masks(key, part):
    return draw_layout(key)[1]


def draw_keys(key, part):
    return audio_keys(key).astype(jnp.bfloat16)


def draw_queries(key, part):
    drawn_rows = jax.random.normal(jax.random.fold_in(key, 31), (VIDEO, HEADS * HEAD_DIM), jnp.float32)
    drawn_rows = jnp.clip(drawn_rows, -6.0, 6.0)
    return drawn_rows.astype(jnp.bfloat16)


def block_levels(stream_key, dims, cuts, least, high):
    gain = 1.0
    for dim, parts in cuts:
        heights = jax.random.uniform(jax.random.fold_in(jax.random.fold_in(stream_key, 6), dim), (parts,), jnp.float32, least / len(cuts), high / len(cuts))
        gain = gain * jnp.repeat(jnp.exp(heights), dims[dim] // parts).reshape((-1,) + (1,) * (len(dims) - 1 - dim))
    return gain


def scatter_about(stream_key, dims, deviation, most, cuts=(), kind=jnp.bfloat16):
    entries = deviation * jax.random.normal(stream_key, dims, jnp.float32)
    if cuts:
        entries = entries * block_levels(stream_key, dims, cuts, -0.22, 0.18)
    return jnp.clip(entries, -most, most).astype(kind)


def setup_inputs(seed: int = 0) -> dict:
    arg_keys = jax.random.split(jax.random.key(seed), 8)
    queries = draw_queries(jax.random.fold_in(arg_keys[7], 71), 0)
    keys = draw_keys(jax.random.fold_in(arg_keys[7], 71), 0)
    values = scatter_about(arg_keys[2], (AUDIO, INNER), 1.0, 6.0, ((0, 16), (1, 2)))
    out_weight = scatter_about(arg_keys[3], (INNER, D), INNER ** -0.5, 0.109375, ((0, 2),))
    out_grad = scatter_about(arg_keys[4], (VIDEO, D), 1.0, 6.0, ((0, 16), (1, 2)))
    align_lists = draw_align_lists(jax.random.fold_in(arg_keys[7], 71), 0)
    block_masks = draw_block_masks(jax.random.fold_in(arg_keys[7], 71), 0)
    return {"queries": queries, "keys": keys, "values": values, "out_weight": out_weight, "out_grad": out_grad, "align_lists": align_lists, "block_masks": block_masks}


def round_keep(value):
    return lax.optimization_barrier(value.astype(jnp.bfloat16)).astype(jnp.float32)

def tile_probs(query_tile, key_rows, live_tile):
    score_scale = 1.0 / math.sqrt(HEAD_DIM)
    query_heads = query_tile.astype(jnp.float32).reshape(TILE, HEADS, HEAD_DIM)
    key_heads = key_rows.astype(jnp.float32).reshape(BLOCKS * TILE, HEADS, HEAD_DIM)
    scores = jnp.einsum('qhd,khd->hqk', query_heads, key_heads) * score_scale
    key_live = jnp.repeat(live_tile, TILE)
    scores = jnp.where(key_live[None, None, :], scores, -jnp.inf)
    row_top = lax.optimization_barrier(jnp.max(scores, -1, keepdims=True))
    exp_scores = jnp.exp(scores - row_top)
    return exp_scores / lax.optimization_barrier(jnp.sum(exp_scores, -1, keepdims=True))

def reference(queries, keys, values, out_weight, out_grad, align_lists, block_masks):
    inner = HEADS * HEAD_DIM
    score_scale = 1.0 / math.sqrt(HEAD_DIM)
    tile_slab = jnp.arange(VTILES, dtype=jnp.int32) // VT_DEV
    live_block = block_masks >= 0
    picked = jnp.take_along_axis(align_lists[tile_slab], jnp.maximum(block_masks, 0), axis=1)
    picked = jnp.where(live_block, picked, 0).astype(jnp.int32)
    key_tiles = keys.reshape(ATILES, TILE, inner)
    value_tiles = values.reshape(ATILES, TILE, inner)
    query_tiles = queries.reshape(VTILES, TILE, inner)

    def forward_tile(operands):
        query_tile, picked_tile, live_tile = operands
        soft_probs = tile_probs(query_tile, key_tiles[picked_tile], live_tile)
        weights = round_keep(soft_probs)
        value_heads = value_tiles[picked_tile].astype(jnp.float32).reshape(BLOCKS * TILE, HEADS, HEAD_DIM)
        return jnp.einsum('hqk,khd->qhd', weights, value_heads).astype(jnp.bfloat16).reshape(TILE, inner)
    attended = lax.map(forward_tile, (query_tiles, picked, live_block)).reshape(VIDEO, inner)
    group_cols = inner // N_HEAD
    mixed_sum = jnp.zeros((VIDEO, D), jnp.float32)
    for group_index in range(N_HEAD):
        low = group_index * group_cols
        partial_sum = jnp.dot(attended[:, low:low + group_cols], out_weight[low:low + group_cols], preferred_element_type=jnp.float32)
        mixed_sum = mixed_sum + round_keep(partial_sum)
    mixed = mixed_sum.astype(jnp.bfloat16)
    grad_attended = jnp.dot(out_grad, out_weight.T, preferred_element_type=jnp.float32).astype(jnp.bfloat16)
    grad_tiles = grad_attended.reshape(VTILES, TILE, inner)
    attended_tiles = attended.reshape(VTILES, TILE, inner)

    def backward_tile(sums_carry, operands):
        key_sum, value_sum = sums_carry
        query_tile, grad_tile, attended_tile, picked_tile, live_tile = operands
        key_rows = key_tiles[picked_tile]
        value_rows = value_tiles[picked_tile]
        soft_probs = tile_probs(query_tile, key_rows, live_tile)
        weights = round_keep(soft_probs)
        query_heads = query_tile.astype(jnp.float32).reshape(TILE, HEADS, HEAD_DIM)
        key_heads = key_rows.astype(jnp.float32).reshape(BLOCKS * TILE, HEADS, HEAD_DIM)
        value_heads = value_rows.astype(jnp.float32).reshape(BLOCKS * TILE, HEADS, HEAD_DIM)
        grad_heads = grad_tile.astype(jnp.float32).reshape(TILE, HEADS, HEAD_DIM)
        attended_heads = attended_tile.astype(jnp.float32).reshape(TILE, HEADS, HEAD_DIM)
        row_delta = lax.optimization_barrier(jnp.sum(grad_heads * attended_heads, -1))
        grad_probs = jnp.einsum('qhd,khd->hqk', grad_heads, value_heads)
        grad_scores = round_keep(soft_probs * (grad_probs - row_delta.T[:, :, None]))
        query_grad = (jnp.einsum('hqk,khd->qhd', grad_scores, key_heads) * score_scale).astype(jnp.bfloat16).reshape(TILE, inner)
        key_terms = (jnp.einsum('hqk,qhd->khd', grad_scores, query_heads) * score_scale).reshape(BLOCKS, TILE, inner)
        value_terms = jnp.einsum('hqk,qhd->khd', weights, grad_heads).reshape(BLOCKS, TILE, inner)
        keep_block = live_tile[:, None, None]
        key_sum = key_sum.at[picked_tile].add(jnp.where(keep_block, key_terms, jnp.zeros_like(key_terms)))
        value_sum = value_sum.at[picked_tile].add(jnp.where(keep_block, value_terms, jnp.zeros_like(value_terms)))
        return ((key_sum, value_sum), query_grad)
    zero_sum = jnp.zeros((ATILES, TILE, inner), jnp.float32)
    (key_sum, value_sum), query_grad = lax.scan(backward_tile, (zero_sum, zero_sum), (query_tiles, grad_tiles, attended_tiles, picked, live_block))
    key_grad = key_sum.reshape(AUDIO, inner).astype(jnp.bfloat16)
    value_grad = value_sum.reshape(AUDIO, inner).astype(jnp.bfloat16)
    return (mixed, query_grad.reshape(VIDEO, inner), key_grad, value_grad)
```

```python
import functools
import math

import jax
import jax.numpy as jnp
from jax import lax
from jax.experimental import pallas as pl
from jax.experimental.pallas import tpu as pltpu
from jax.sharding import PartitionSpec as P

HD = 128
TILE = 128
GROUP = 4
LIST = 4
BLOCKS = 3
MESH = pl.DeviceIdType.MESH
NT = (((1,), (1,)), ((), ()))
TN = (((0,), (0,)), ((), ()))
AT_S2, AT_S3, AT_CMP, AT_RZ, AT_R1, AT_FIN = 1, 2, 3, 4, 5, 6
F32 = jnp.float32
BF16 = jnp.bfloat16


def kernel(
    n_tm, n_head, heads, rows,
    align, masks, q_hbm, k_hbm, v_hbm, w_hbm, og_hbm,
    mixed_ref, qg_ref, kg_ref, vg_ref,
    q, w, og, att, bias, kcat, vcat,
    kv, zprev, znext, s3buf,
    own, r3send, r3recv, to_prev, to_next, of_next, of_prev, r1send, r1recv,
    msend, mrecv, mown,
    loc_sem, kv_sem, og_send, og_recv, m_send, m_recv,
    s1_send, s1_recv, z_send, z_recv, s3_send, s3_recv,
    r3_ssem, r3_rsem, zb_send, zb_recv, r1_ssem, r1_rsem,
):
    scale = 1.0 / math.sqrt(HD)
    me = lax.axis_index("tm")
    hd = lax.axis_index("head")
    cols = heads * HD
    planes = n_tm // GROUP
    plane = me // GROUP
    p = me % GROUP
    dx = 1 - 2 * (p % 2)
    dy = 2 - 4 * (p // 2)
    has_prev = plane > 0
    has_next = plane < planes - 1

    def sides(c):
        t = c % 2
        d1 = dx * (1 - t) + dy * t
        d2 = dy * (1 - t) + dx * t
        return d1, d2

    def flags(dest, r):
        prev = jnp.int32(0)
        nxt = jnp.int32(0)
        for s in range(LIST):
            a = align[dest, s]
            hit = jnp.logical_and(a >= 0, lax.rem(a + GROUP, GROUP) == r)
            pa = lax.div(a + GROUP, GROUP) - 1
            prev = jnp.where(jnp.logical_and(hit, pa < plane), 1, prev)
            nxt = jnp.where(jnp.logical_and(hit, pa > plane), 1, nxt)
        return prev, nxt

    def rcopy(src, dst, ss, rs, dev):
        return pltpu.make_async_remote_copy(
            src_ref=src, dst_ref=dst, send_sem=ss, recv_sem=rs,
            device_id=dev, device_id_type=MESH,
        )

    def s1_copy(c):
        d1, _ = sides(c)
        return rcopy(kv.at[c, 0], kv.at[c, 1], s1_send.at[c], s1_recv.at[c], {"tm": me + d1})

    def s3_copy(c):
        _, d2 = sides(c)
        return rcopy(
            s3buf.at[c], kv.at[c, pl.ds(2, 2)], s3_send.at[c], s3_recv.at[c], {"tm": me + d2}
        )

    def r3_copy(c):
        _, d2 = sides(c)
        return rcopy(r3send.at[c], r3recv.at[c], r3_ssem.at[c], r3_rsem.at[c], {"tm": me + d2})

    def r1_copy(c):
        d1, _ = sides(c)
        return rcopy(r1send.at[c], r1recv.at[c], r1_ssem.at[c], r1_rsem.at[c], {"tm": me + d1})

    def z_copies(c):
        d1, d2 = sides(c)
        out = []
        for j in range(2):
            r = p + (d1 if j else 0)
            up = jnp.logical_or(r > p, r > p + d2)
            down = jnp.logical_or(r < p, r < p + d2)
            out.append((
                jnp.logical_and(up, has_next),
                rcopy(kv.at[c, j], zprev.at[c, j], z_send.at[c, j], z_recv.at[c, j],
                      {"tm": me + GROUP}),
                jnp.logical_and(up, has_prev),
            ))
            out.append((
                jnp.logical_and(down, has_prev),
                rcopy(kv.at[c, j], znext.at[c, j], z_send.at[c, 2 + j], z_recv.at[c, 2 + j],
                      {"tm": me - GROUP}),
                jnp.logical_and(down, has_next),
            ))
        return out

    def zb_copies(c):
        d1, d2 = sides(c)
        out = []
        for j in range(2):
            r = p + (d1 if j else 0)
            up = jnp.logical_or(r > p, r > p + d2)
            down = jnp.logical_or(r < p, r < p + d2)
            out.append((
                jnp.logical_and(up, has_prev),
                rcopy(to_prev.at[c, j], of_next.at[c, j], zb_send.at[c, j], zb_recv.at[c, j],
                      {"tm": me - GROUP}),
                jnp.logical_and(up, has_next),
            ))
            out.append((
                jnp.logical_and(down, has_next),
                rcopy(to_next.at[c, j], of_prev.at[c, j], zb_send.at[c, 2 + j],
                      zb_recv.at[c, 2 + j], {"tm": me + GROUP}),
                jnp.logical_and(down, has_prev),
            ))
        return out

    def kv_copies(c):
        at = pl.ds(pl.multiple_of(c * HD, HD), HD)
        return (
            pltpu.make_async_copy(k_hbm.at[:, at], kv.at[c, 0, 0], kv_sem.at[c, 0]),
            pltpu.make_async_copy(v_hbm.at[:, at], kv.at[c, 0, 1], kv_sem.at[c, 1]),
        )

    def start_kv(c, carry):
        for copy in kv_copies(c):
            copy.start()
        return carry

    lax.fori_loop(0, heads, start_kv, 0)

    og_own = pl.ds(pl.multiple_of(hd * cols, HD), cols)
    local = (
        pltpu.make_async_copy(og_hbm, og.at[:, og_own], loc_sem.at[0]),
        pltpu.make_async_copy(q_hbm, q, loc_sem.at[1]),
        pltpu.make_async_copy(w_hbm, w, loc_sem.at[2]),
    )
    for copy in local:
        copy.start()

    barrier = pltpu.get_barrier_semaphore()
    pl.semaphore_signal(barrier, inc=1, device_id={"tm": me + dx}, device_id_type=MESH)
    pl.semaphore_signal(barrier, inc=1, device_id={"tm": me + dy}, device_id_type=MESH)

    @pl.when(has_prev)
    def _():
        pl.semaphore_signal(barrier, inc=1, device_id={"tm": me - GROUP}, device_id_type=MESH)

    @pl.when(has_next)
    def _():
        pl.semaphore_signal(barrier, inc=1, device_id={"tm": me + GROUP}, device_id_type=MESH)

    for k in range(1, n_head):
        pl.semaphore_signal(
            barrier, inc=1, device_id={"head": (hd + k) % n_head}, device_id_type=MESH
        )

    row = lax.broadcasted_iota(jnp.int32, (rows, GROUP * TILE), 0)
    col = lax.broadcasted_iota(jnp.int32, (rows, GROUP * TILE), 1)
    for t in range(2):
        d1, d2 = sides(t)
        residues = (p, p + d1, p + d2, p + d1 + d2)
        total = jnp.full((rows, GROUP * TILE), -1e30, F32)
        for i in range(rows // TILE):
            for j, r in enumerate(residues):
                live = jnp.float32(-1e30)
                for b in range(BLOCKS):
                    m = masks[i, b]
                    for s in range(LIST):
                        a = align[me, s]
                        hit = jnp.logical_and(m == s, lax.rem(a + GROUP, GROUP) == r)
                        live = jnp.where(hit, jnp.float32(0.0), live)
                here = jnp.logical_and(row // TILE == i, col // TILE == j)
                total = jnp.where(here, live, total)
        bias[t] = total

    near = 2 + (n_head - 1) + jnp.where(has_prev, 1, 0) + jnp.where(has_next, 1, 0)
    pl.semaphore_wait(barrier, near)

    def og_copy(k):
        return rcopy(
            og_hbm, og.at[:, og_own], og_send.at[k - 1], og_recv.at[k - 1],
            {"head": (hd + k) % n_head},
        )

    def og_arrival(k):
        src = (hd - k + n_head) % n_head
        return rcopy(
            og_hbm, og.at[:, pl.ds(pl.multiple_of(src * cols, HD), cols)],
            og_send.at[k - 1], og_recv.at[k - 1], {"head": (hd + k) % n_head},
        )

    def pick(c, j, prev, nxt):
        mine = kv[c, j].astype(F32)
        before = zprev[c, j].astype(F32)
        after = znext[c, j].astype(F32)
        return jnp.where(prev > 0, before, jnp.where(nxt > 0, after, mine)).astype(BF16)

    def step(k, carry):
        def stage(skew, body):
            c = k - skew
            pl.when(jnp.logical_and(c >= 0, c < heads))(lambda: body(c))

        def s1(c):
            for copy in kv_copies(c):
                copy.wait()
            s1_copy(c).start()

        def s2(c):
            s1_copy(c).wait_recv()
            for out, copy, _ in z_copies(c):
                pl.when(out)(copy.start)

        def s3(c):
            for _, copy, come in z_copies(c):
                pl.when(come)(copy.wait_recv)
            d1, d2 = sides(c)
            for j in range(2):
                prev, nxt = flags(me + d2, p + (d1 if j else 0))
                s3buf[c, j] = pick(c, j, prev, nxt)
            s3_copy(c).start()

        def cmp(c):
            @pl.when(c == 0)
            def _():
                for copy in local:
                    copy.wait()
                for kk in range(1, n_head):
                    og_arrival(kk).wait_recv()

            d1, d2 = sides(c)
            at = pl.ds(pl.multiple_of(c * HD, HD), HD)
            ga = lax.dot_general(og[...], w[at, :], NT, preferred_element_type=F32).astype(BF16)
            prev, nxt = flags(me, p + d1)
            chosen = pick(c, 1, prev, nxt)
            kcat[0:TILE] = kv[c, 0, 0]
            vcat[0:TILE] = kv[c, 0, 1]
            kcat[TILE:2 * TILE] = chosen[0]
            vcat[TILE:2 * TILE] = chosen[1]
            s3_copy(c).wait_recv()
            for j in (2, 3):
                kcat[j * TILE:(j + 1) * TILE] = kv[c, j, 0]
                vcat[j * TILE:(j + 1) * TILE] = kv[c, j, 1]
            qh = q[:, at]
            kh = kcat[...]
            vh = vcat[...]
            scores = lax.dot_general(qh, kh, NT, preferred_element_type=F32) * scale
            scores = scores + bias[c % 2]
            top = jnp.max(scores, -1, keepdims=True)
            e = jnp.exp(scores - top)
            probs = e * (1.0 / jnp.sum(e, -1, keepdims=True))
            weights = probs.astype(BF16)
            attended = jnp.dot(weights, vh, preferred_element_type=F32).astype(BF16)
            att[:, at] = attended
            delta = jnp.sum(ga.astype(F32) * attended.astype(F32), -1, keepdims=True)
            gp = lax.dot_general(ga, vh, NT, preferred_element_type=F32)
            gs = (probs * (gp - delta)).astype(BF16)
            kt = lax.dot_general(gs, qh, TN, preferred_element_type=F32) * scale
            vt = lax.dot_general(weights, ga, TN, preferred_element_type=F32)
            for j in range(2):
                r3send[c, j, 0] = kt[(2 + j) * TILE:(3 + j) * TILE].astype(BF16)
                r3send[c, j, 1] = vt[(2 + j) * TILE:(3 + j) * TILE].astype(BF16)
            r3_copy(c).start()
            for j in range(2):
                own[c, j, 0] = kt[j * TILE:(j + 1) * TILE]
                own[c, j, 1] = vt[j * TILE:(j + 1) * TILE]
            qg = jnp.dot(gs, kh, preferred_element_type=F32) * scale
            qg_ref[:, at] = qg.astype(BF16)

        def rz(c):
            d1, d2 = sides(c)
            r3_copy(c).wait_recv()
            for j in range(2):
                r = p + (d1 if j else 0)
                mp, mn = flags(me, r)
                op, on = flags(me + d2, r)
                mp, mn, op, on = (x.astype(F32) for x in (mp, mn, op, on))
                mine = own[c, j]
                other = r3recv[c, j].astype(F32)
                to_prev[c, j] = (mine * mp + other * op).astype(BF16)
                to_next[c, j] = (mine * mn + other * on).astype(BF16)
                own[c, j] = mine * (1.0 - mp - mn) + other * (1.0 - op - on)
            for out, copy, _ in zb_copies(c):
                pl.when(out)(copy.start)

        def r1(c):
            copies = zb_copies(c)
            for _, copy, come in copies:
                pl.when(come)(copy.wait_recv)
            sums = []
            for j in range(2):
                total = own[c, j]
                total = total + jnp.where(copies[2 * j][2], of_next[c, j].astype(F32), 0.0)
                total = total + jnp.where(copies[2 * j + 1][2], of_prev[c, j].astype(F32), 0.0)
                sums.append(total)
            r1send[c] = sums[1].astype(BF16)
            r1_copy(c).start()
            own[c, 0] = sums[0]

        def fin(c):
            r1_copy(c).wait_recv()
            at = pl.ds(pl.multiple_of(c * HD, HD), HD)
            kg_ref[:, at] = (own[c, 0, 0] + r1recv[c, 0].astype(F32)).astype(BF16)
            vg_ref[:, at] = (own[c, 0, 1] + r1recv[c, 1].astype(F32)).astype(BF16)

        stage(0, s1)

        @pl.when(k == 0)
        def _():
            for kk in range(1, n_head):
                og_copy(kk).start()

        stage(AT_S2, s2)
        stage(AT_S3, s3)
        stage(AT_CMP, cmp)

        @pl.when(k == heads + AT_CMP)
        def _():
            mix()

        stage(AT_RZ, rz)
        stage(AT_R1, r1)
        stage(AT_FIN, fin)
        return carry

    block = 256 if cols % 256 == 0 else 128

    def m_copy(k):
        return rcopy(
            msend.at[k - 1], mrecv.at[k - 1], m_send.at[k - 1], m_recv.at[k - 1],
            {"head": (hd + k) % n_head},
        )

    def mix():
        for k in list(range(1, n_head)) + [0]:
            base = ((hd + k) % n_head) * cols
            out = msend.at[k - 1] if k else mown

            def one(n, carry, base=base, out=out):
                src = pl.ds(pl.multiple_of(base + n * block, 128), block)
                dst = pl.ds(pl.multiple_of(n * block, 128), block)
                part = jnp.dot(att[...], w[:, src], preferred_element_type=F32)
                out[:, dst] = part.astype(BF16)
                return carry

            lax.fori_loop(0, cols // block, one, 0)
            if k:
                m_copy(k).start()

    lax.fori_loop(0, heads + AT_FIN, step, 0)

    for k in range(1, n_head):
        m_copy(k).wait_recv()
    total = mown[...].astype(F32)
    for k in range(1, n_head):
        total = total + mrecv[k - 1].astype(F32)
    mixed_ref[...] = total.astype(BF16)

    def drain(c, carry):
        s1_copy(c).wait_send()
        s3_copy(c).wait_send()
        r3_copy(c).wait_send()
        r1_copy(c).wait_send()
        for out, copy, _ in z_copies(c) + zb_copies(c):
            pl.when(out)(copy.wait_send)
        return carry

    lax.fori_loop(0, heads, drain, 0)
    for k in range(1, n_head):
        og_copy(k).wait_send()
        m_copy(k).wait_send()


def local(n_tm, n_head, queries, keys, values, out_weight, out_grad, align_lists, block_masks):
    rows, cols = queries.shape
    heads = cols // HD
    width = out_weight.shape[1]
    others = max(n_head - 1, 1)
    pair = (2, TILE, HD)
    hbm = pl.BlockSpec(memory_space=pl.ANY)
    smem = pl.BlockSpec(memory_space=pltpu.SMEM)
    vmem = pl.BlockSpec(memory_space=pltpu.VMEM)
    dma = pltpu.SemaphoreType.DMA
    V = pltpu.VMEM
    return pl.pallas_call(
        functools.partial(kernel, n_tm, n_head, heads, rows),
        out_shape=(
            jax.ShapeDtypeStruct((rows, cols), BF16),
            jax.ShapeDtypeStruct((rows, cols), BF16),
            jax.ShapeDtypeStruct(keys.shape, BF16),
            jax.ShapeDtypeStruct(keys.shape, BF16),
        ),
        in_specs=[smem, smem, hbm, hbm, hbm, hbm, hbm],
        out_specs=(vmem, vmem, vmem, vmem),
        scratch_shapes=[
            V((rows, cols), BF16),
            V((cols, width), BF16),
            V((rows, width), BF16),
            V((rows, cols), BF16),
            V((2, rows, GROUP * TILE), F32),
            V((GROUP * TILE, HD), BF16),
            V((GROUP * TILE, HD), BF16),
            V((heads, 4) + pair, BF16),
            V((heads, 2) + pair, BF16),
            V((heads, 2) + pair, BF16),
            V((heads, 2) + pair, BF16),
            V((heads, 2) + pair, F32),
            V((heads, 2) + pair, BF16),
            V((heads, 2) + pair, BF16),
            V((heads, 2) + pair, BF16),
            V((heads, 2) + pair, BF16),
            V((heads, 2) + pair, BF16),
            V((heads, 2) + pair, BF16),
            V((heads,) + pair, BF16),
            V((heads,) + pair, BF16),
            V((others, rows, cols), BF16),
            V((others, rows, cols), BF16),
            V((rows, cols), BF16),
            dma((3,)),
            dma((heads, 2)),
            dma((others,)),
            dma((others,)),
            dma((others,)),
            dma((others,)),
            dma((heads,)),
            dma((heads,)),
            dma((heads, 4)),
            dma((heads, 4)),
            dma((heads,)),
            dma((heads,)),
            dma((heads,)),
            dma((heads,)),
            dma((heads, 4)),
            dma((heads, 4)),
            dma((heads,)),
            dma((heads,)),
        ],
        compiler_params=pltpu.CompilerParams(
            collective_id=0, has_side_effects=True, vmem_limit_bytes=56 * 1024 * 1024
        ),
        cost_estimate=pl.CostEstimate(
            flops=4 * rows * cols * width + 12 * rows * GROUP * TILE * cols,
            bytes_accessed=2 * cols * width, transcendentals=rows * GROUP * TILE * heads,
        ),
    )(align_lists, block_masks, queries, keys, values, out_weight, out_grad)


def solution(mesh):
    split = P("tm", "head")
    return jax.shard_map(
        functools.partial(local, mesh.shape["tm"], mesh.shape["head"]),
        mesh=mesh,
        in_specs=(split, split, split, P("head", None), split, P(), P("tm", None)),
        out_specs=(split, split, split, split),
        check_vma=False,
    )
```

```python
import functools
import math

import jax
import jax.numpy as jnp
from jax import lax
from jax.experimental import pallas as pl
from jax.experimental.pallas import tpu as pltpu
from jax.sharding import PartitionSpec as P

HD = 128
TILE = 128
GROUP = 4
LIST = 4
BLOCKS = 3
MESH = pl.DeviceIdType.MESH
NT = (((1,), (1,)), ((), ()))
TN = (((0,), (0,)), ((), ()))
LEAD = 4
AT_S2, AT_S3, AT_CMP, AT_RZ, AT_R1, AT_FIN = 1, 2, 3, 4, 5, 6
F32 = jnp.float32
BF16 = jnp.bfloat16


def kernel(
    n_tm, n_head, heads, rows,
    align, masks, q_hbm, k_hbm, v_hbm, w_hbm, og_hbm,
    mixed_hbm, qg_hbm, kg_hbm, vg_hbm,
    mixed_ref, qg_ref, kg_ref, vg_ref, q, w, og, ga_all, att, bias, kcat, vcat,
    kv, zprev, znext, s3buf,
    own, r3send, r3recv, to_prev, to_next, of_next, of_prev, r1send, r1recv,
    msend, mrecv, mown,
    out_sem, loc_sem, kv_sem, og_send, og_recv, m_send, m_recv,
    s1_send, s1_recv, z_send, z_recv, s3_send, s3_recv,
    r3_ssem, r3_rsem, zb_send, zb_recv, r1_ssem, r1_rsem,
):
    scale = 1.0 / math.sqrt(HD)
    me = lax.axis_index("tm")
    hd = lax.axis_index("head")
    cols = heads * HD
    planes = n_tm // GROUP
    plane = me // GROUP
    p = me % GROUP
    dx = 1 - 2 * (p % 2)
    dy = 2 - 4 * (p // 2)
    has_prev = plane > 0
    has_next = plane < planes - 1

    def sides(c):
        t = c % 2
        d1 = dx * (1 - t) + dy * t
        d2 = dy * (1 - t) + dx * t
        return d1, d2

    def flags(dest, r):
        prev = jnp.int32(0)
        nxt = jnp.int32(0)
        for s in range(LIST):
            a = align[s, dest]
            hit = jnp.logical_and(a >= 0, lax.rem(a + GROUP, GROUP) == r)
            pa = lax.div(a + GROUP, GROUP) - 1
            prev = jnp.where(jnp.logical_and(hit, pa < plane), 1, prev)
            nxt = jnp.where(jnp.logical_and(hit, pa > plane), 1, nxt)
        return prev, nxt

    def rcopy(src, dst, ss, rs, dev):
        return pltpu.make_async_remote_copy(
            src_ref=src, dst_ref=dst, send_sem=ss, recv_sem=rs,
            device_id=dev, device_id_type=MESH,
        )

    def s1_copy(c):
        d1, _ = sides(c)
        return rcopy(kv.at[c, 0], kv.at[c, 1], s1_send.at[c], s1_recv.at[c], {"tm": me + d1})

    def s3_copy(c):
        _, d2 = sides(c)
        return rcopy(
            s3buf.at[c], kv.at[c, pl.ds(2, 2)], s3_send.at[c], s3_recv.at[c], {"tm": me + d2}
        )

    def r3_copy(c):
        _, d2 = sides(c)
        return rcopy(r3send.at[c], r3recv.at[c], r3_ssem.at[c], r3_rsem.at[c], {"tm": me + d2})

    def r1_copy(c):
        d1, _ = sides(c)
        return rcopy(r1send.at[c], r1recv.at[c], r1_ssem.at[c], r1_rsem.at[c], {"tm": me + d1})

    def z_copies(c):
        d1, d2 = sides(c)
        out = []
        for j in range(2):
            r = p + (d1 if j else 0)
            up = jnp.logical_or(r > p, r > p + d2)
            down = jnp.logical_or(r < p, r < p + d2)
            out.append((
                jnp.logical_and(up, has_next),
                rcopy(kv.at[c, j], zprev.at[c, j], z_send.at[c, j], z_recv.at[c, j],
                      {"tm": me + GROUP}),
                jnp.logical_and(up, has_prev),
            ))
            out.append((
                jnp.logical_and(down, has_prev),
                rcopy(kv.at[c, j], znext.at[c, j], z_send.at[c, 2 + j], z_recv.at[c, 2 + j],
                      {"tm": me - GROUP}),
                jnp.logical_and(down, has_next),
            ))
        return out

    def zb_copies(c):
        d1, d2 = sides(c)
        out = []
        for j in range(2):
            r = p + (d1 if j else 0)
            up = jnp.logical_or(r > p, r > p + d2)
            down = jnp.logical_or(r < p, r < p + d2)
            out.append((
                jnp.logical_and(up, has_prev),
                rcopy(to_prev.at[c, j], of_next.at[c, j], zb_send.at[c, j], zb_recv.at[c, j],
                      {"tm": me - GROUP}),
                jnp.logical_and(up, has_next),
            ))
            out.append((
                jnp.logical_and(down, has_next),
                rcopy(to_next.at[c, j], of_prev.at[c, j], zb_send.at[c, 2 + j],
                      zb_recv.at[c, 2 + j], {"tm": me + GROUP}),
                jnp.logical_and(down, has_prev),
            ))
        return out

    def kv_copies(c):
        at = pl.ds(pl.multiple_of(c * HD, HD), HD)
        return (
            pltpu.make_async_copy(k_hbm.at[:, at], kv.at[c, 0, 0], kv_sem.at[c, 0]),
            pltpu.make_async_copy(v_hbm.at[:, at], kv.at[c, 0, 1], kv_sem.at[c, 1]),
        )

    def start_kv(c, carry):
        for copy in kv_copies(c):
            copy.start()
        return carry

    lax.fori_loop(0, heads, start_kv, 0)

    og_own = pl.ds(pl.multiple_of(hd * cols, HD), cols)
    local = (
        pltpu.make_async_copy(og_hbm, og.at[:, og_own], loc_sem.at[0]),
        pltpu.make_async_copy(q_hbm, q, loc_sem.at[1]),
        pltpu.make_async_copy(w_hbm, w, loc_sem.at[2]),
    )
    for copy in local:
        copy.start()

    barrier = pltpu.get_barrier_semaphore()
    pl.semaphore_signal(barrier, inc=1, device_id={"tm": me + dx}, device_id_type=MESH)
    pl.semaphore_signal(barrier, inc=1, device_id={"tm": me + dy}, device_id_type=MESH)

    @pl.when(has_prev)
    def _():
        pl.semaphore_signal(barrier, inc=1, device_id={"tm": me - GROUP}, device_id_type=MESH)

    @pl.when(has_next)
    def _():
        pl.semaphore_signal(barrier, inc=1, device_id={"tm": me + GROUP}, device_id_type=MESH)

    for k in range(1, n_head):
        pl.semaphore_signal(
            barrier, inc=1, device_id={"head": (hd + k) % n_head}, device_id_type=MESH
        )

    row = lax.broadcasted_iota(jnp.int32, (rows, GROUP * TILE), 0)
    col = lax.broadcasted_iota(jnp.int32, (rows, GROUP * TILE), 1)
    for t in range(2):
        d1, d2 = sides(t)
        residues = (p, p + d1, p + d2, p + d1 + d2)
        total = jnp.full((rows, GROUP * TILE), -1e30, F32)
        for i in range(rows // TILE):
            for j, r in enumerate(residues):
                live = jnp.float32(-1e30)
                for b in range(BLOCKS):
                    m = masks[i, b]
                    for s in range(LIST):
                        a = align[s, me]
                        hit = jnp.logical_and(m == s, lax.rem(a + GROUP, GROUP) == r)
                        live = jnp.where(hit, jnp.float32(0.0), live)
                here = jnp.logical_and(row // TILE == i, col // TILE == j)
                total = jnp.where(here, live, total)
        bias[t] = total

    near = 2 + (n_head - 1) + jnp.where(has_prev, 1, 0) + jnp.where(has_next, 1, 0)
    pl.semaphore_wait(barrier, near)

    def og_copy(k):
        return rcopy(
            og_hbm, og.at[:, og_own], og_send.at[k - 1], og_recv.at[k - 1],
            {"head": (hd + k) % n_head},
        )

    def og_arrival(k):
        src = (hd - k + n_head) % n_head
        return rcopy(
            og_hbm, og.at[:, pl.ds(pl.multiple_of(src * cols, HD), cols)],
            og_send.at[k - 1], og_recv.at[k - 1], {"head": (hd + k) % n_head},
        )

    def pick(c, j, prev, nxt):
        mine = kv[c, j].astype(F32)
        before = zprev[c, j].astype(F32)
        after = znext[c, j].astype(F32)
        return jnp.where(prev > 0, before, jnp.where(nxt > 0, after, mine)).astype(BF16)

    def step(k, carry):
        def stage(skew, body):
            c = k - skew
            pl.when(jnp.logical_and(c >= 0, c < heads))(lambda: body(c))

        def s1(c):
            for copy in kv_copies(c):
                copy.wait()
            s1_copy(c).start()

        def s2(c):
            s1_copy(c).wait_recv()
            for out, copy, _ in z_copies(c):
                pl.when(out)(copy.start)

        def s3(c):
            for _, copy, come in z_copies(c):
                pl.when(come)(copy.wait_recv)
            d1, d2 = sides(c)
            for j in range(2):
                prev, nxt = flags(me + d2, p + (d1 if j else 0))
                s3buf[c, j] = pick(c, j, prev, nxt)
            s3_copy(c).start()

        def cmp(c):
            d1, d2 = sides(c)
            at = pl.ds(pl.multiple_of(c * HD, HD), HD)
            ga = ga_all[:, at]
            prev, nxt = flags(me, p + d1)
            chosen = pick(c, 1, prev, nxt)
            kcat[0:TILE] = kv[c, 0, 0]
            vcat[0:TILE] = kv[c, 0, 1]
            kcat[TILE:2 * TILE] = chosen[0]
            vcat[TILE:2 * TILE] = chosen[1]
            s3_copy(c).wait_recv()
            for j in (2, 3):
                kcat[j * TILE:(j + 1) * TILE] = kv[c, j, 0]
                vcat[j * TILE:(j + 1) * TILE] = kv[c, j, 1]
            qh = q[:, at]
            kh = kcat[...]
            vh = vcat[...]
            scores = lax.dot_general(qh, kh, NT, preferred_element_type=F32) * scale
            scores = scores + bias[c % 2]
            top = jnp.max(scores, -1, keepdims=True)
            e = jnp.exp(scores - top)
            probs = e * (1.0 / jnp.sum(e, -1, keepdims=True))
            weights = probs.astype(BF16)
            attended = jnp.dot(weights, vh, preferred_element_type=F32).astype(BF16)
            att[:, at] = attended
            delta = jnp.sum(ga.astype(F32) * attended.astype(F32), -1, keepdims=True)
            gp = lax.dot_general(ga, vh, NT, preferred_element_type=F32)
            gs = (probs * (gp - delta)).astype(BF16)
            kt = lax.dot_general(gs, qh, TN, preferred_element_type=F32) * scale
            vt = lax.dot_general(weights, ga, TN, preferred_element_type=F32)
            for j in range(2):
                r3send[c, j, 0] = kt[(2 + j) * TILE:(3 + j) * TILE].astype(BF16)
                r3send[c, j, 1] = vt[(2 + j) * TILE:(3 + j) * TILE].astype(BF16)
            r3_copy(c).start()
            for j in range(2):
                own[c, j, 0] = kt[j * TILE:(j + 1) * TILE]
                own[c, j, 1] = vt[j * TILE:(j + 1) * TILE]
            qg = jnp.dot(gs, kh, preferred_element_type=F32) * scale
            qg_ref[:, at] = qg.astype(BF16)

        def rz(c):
            d1, d2 = sides(c)
            r3_copy(c).wait_recv()
            for j in range(2):
                r = p + (d1 if j else 0)
                mp, mn = flags(me, r)
                op, on = flags(me + d2, r)
                mp, mn, op, on = (x.astype(F32) for x in (mp, mn, op, on))
                mine = own[c, j]
                other = r3recv[c, j].astype(F32)
                to_prev[c, j] = (mine * mp + other * op).astype(BF16)
                to_next[c, j] = (mine * mn + other * on).astype(BF16)
                own[c, j] = mine * (1.0 - mp - mn) + other * (1.0 - op - on)
            for out, copy, _ in zb_copies(c):
                pl.when(out)(copy.start)

        def r1(c):
            copies = zb_copies(c)
            for _, copy, come in copies:
                pl.when(come)(copy.wait_recv)
            sums = []
            for j in range(2):
                total = own[c, j]
                total = total + jnp.where(copies[2 * j][2], of_next[c, j].astype(F32), 0.0)
                total = total + jnp.where(copies[2 * j + 1][2], of_prev[c, j].astype(F32), 0.0)
                sums.append(total)
            r1send[c] = sums[1].astype(BF16)
            r1_copy(c).start()
            own[c, 0] = sums[0]

        def fin(c):
            r1_copy(c).wait_recv()
            at = pl.ds(pl.multiple_of(c * HD, HD), HD)
            kg_ref[:, at] = (own[c, 0, 0] + r1recv[c, 0].astype(F32)).astype(BF16)
            vg_ref[:, at] = (own[c, 0, 1] + r1recv[c, 1].astype(F32)).astype(BF16)

        @pl.when(k == 0)
        def _():
            for kk in range(1, n_head):
                og_copy(kk).start()
            for c in range(lead):
                s1(c)

        stage(-lead, s1)
        stage(AT_S2, s2)

        @pl.when(k == AT_S2)
        def _():
            for copy in local:
                copy.wait()
            for kk in range(1, n_head):
                og_arrival(kk).wait_recv()
            grads(0, blocks // 2)

        stage(AT_S3, s3)

        @pl.when(k == AT_S3)
        def _():
            grads(blocks // 2, blocks)

        stage(AT_CMP, cmp)

        @pl.when(k == heads + AT_CMP)
        def _():
            outs[1].start()
            for kk in range(1, n_head):
                mix(kk)

        stage(AT_RZ, rz)

        @pl.when(k == heads + AT_CMP)
        def _():
            mix(0)

        stage(AT_R1, r1)

        @pl.when(k == heads + AT_FIN - 1)
        def _():
            for kk in range(1, n_head):
                m_copy(kk).wait_recv()
            total = mown[...].astype(F32)
            for kk in range(1, n_head):
                total = total + mrecv[kk - 1].astype(F32)
            mixed_ref[...] = total.astype(BF16)
            outs[0].start()

        stage(AT_FIN, fin)
        return carry

    lead = min(LEAD, heads)
    block = 256 if cols % 256 == 0 else 128
    blocks = cols // block
    outs = tuple(
        pltpu.make_async_copy(src, dst, out_sem.at[i])
        for i, (src, dst) in enumerate((
            (mixed_ref, mixed_hbm), (qg_ref, qg_hbm), (kg_ref, kg_hbm), (vg_ref, vg_hbm),
        ))
    )

    def grads(first, last):
        def one(n, carry):
            at = pl.ds(pl.multiple_of(n * block, 128), block)
            ga = lax.dot_general(og[...], w[at, :], NT, preferred_element_type=F32)
            ga_all[:, at] = ga.astype(BF16)
            return carry

        lax.fori_loop(first, last, one, 0)

    def m_copy(k):
        return rcopy(
            msend.at[k - 1], mrecv.at[k - 1], m_send.at[k - 1], m_recv.at[k - 1],
            {"head": (hd + k) % n_head},
        )

    def mix(k):
        base = ((hd + k) % n_head) * cols
        out = msend.at[k - 1] if k else mown

        def one(n, carry):
            src = pl.ds(pl.multiple_of(base + n * block, 128), block)
            dst = pl.ds(pl.multiple_of(n * block, 128), block)
            part = jnp.dot(att[...], w[:, src], preferred_element_type=F32)
            out[:, dst] = part.astype(BF16)
            return carry

        lax.fori_loop(0, blocks, one, 0)
        if k:
            m_copy(k).start()

    lax.fori_loop(0, heads + AT_FIN, step, 0)

    outs[2].start()
    outs[3].start()

    def drain(c, carry):
        s1_copy(c).wait_send()
        s3_copy(c).wait_send()
        r3_copy(c).wait_send()
        r1_copy(c).wait_send()
        for out, copy, _ in z_copies(c) + zb_copies(c):
            pl.when(out)(copy.wait_send)
        return carry

    lax.fori_loop(0, heads, drain, 0)
    for k in range(1, n_head):
        og_copy(k).wait_send()
        m_copy(k).wait_send()
    for copy in outs:
        copy.wait()


def hand_on(*refs):
    n = len(refs) // 2
    sems = refs[-1]
    copies = [pltpu.make_async_copy(refs[i], refs[n + i], sems.at[i]) for i in range(n)]
    for copy in copies:
        copy.start()
    for copy in copies:
        copy.wait()


def local(n_tm, n_head, queries, keys, values, out_weight, out_grad, align_lists, block_masks):
    rows, cols = queries.shape
    heads = cols // HD
    width = out_weight.shape[1]
    others = max(n_head - 1, 1)
    pair = (2, TILE, HD)
    hbm = pl.BlockSpec(memory_space=pl.ANY)
    smem = pl.BlockSpec(memory_space=pltpu.SMEM)
    dma = pltpu.SemaphoreType.DMA
    V = pltpu.VMEM
    shapes = (
        jax.ShapeDtypeStruct((rows, cols), BF16),
        jax.ShapeDtypeStruct((rows, cols), BF16),
        jax.ShapeDtypeStruct(keys.shape, BF16),
        jax.ShapeDtypeStruct(keys.shape, BF16),
    )
    results = pl.pallas_call(
        functools.partial(kernel, n_tm, n_head, heads, rows),
        out_shape=shapes,
        in_specs=[smem, smem, hbm, hbm, hbm, hbm, hbm],
        out_specs=(hbm,) * 4,
        scratch_shapes=[
            V((rows, cols), BF16),
            V((rows, cols), BF16),
            V(keys.shape, BF16),
            V(keys.shape, BF16),
            V((rows, cols), BF16),
            V((cols, width), BF16),
            V((rows, width), BF16),
            V((rows, cols), BF16),
            V((rows, cols), BF16),
            V((2, rows, GROUP * TILE), F32),
            V((GROUP * TILE, HD), BF16),
            V((GROUP * TILE, HD), BF16),
            V((heads, 4) + pair, BF16),
            V((heads, 2) + pair, BF16),
            V((heads, 2) + pair, BF16),
            V((heads, 2) + pair, BF16),
            V((heads, 2) + pair, F32),
            V((heads, 2) + pair, BF16),
            V((heads, 2) + pair, BF16),
            V((heads, 2) + pair, BF16),
            V((heads, 2) + pair, BF16),
            V((heads, 2) + pair, BF16),
            V((heads, 2) + pair, BF16),
            V((heads,) + pair, BF16),
            V((heads,) + pair, BF16),
            V((others, rows, cols), BF16),
            V((others, rows, cols), BF16),
            V((rows, cols), BF16),
            dma((4,)),
            dma((3,)),
            dma((heads, 2)),
            dma((others,)),
            dma((others,)),
            dma((others,)),
            dma((others,)),
            dma((heads,)),
            dma((heads,)),
            dma((heads, 4)),
            dma((heads, 4)),
            dma((heads,)),
            dma((heads,)),
            dma((heads,)),
            dma((heads,)),
            dma((heads, 4)),
            dma((heads, 4)),
            dma((heads,)),
            dma((heads,)),
        ],
        compiler_params=pltpu.CompilerParams(
            collective_id=0, has_side_effects=True, vmem_limit_bytes=56 * 1024 * 1024
        ),
        cost_estimate=pl.CostEstimate(
            flops=4 * rows * cols * width + 12 * rows * GROUP * TILE * cols,
            bytes_accessed=2 * cols * width, transcendentals=rows * GROUP * TILE * heads,
        ),
    )(align_lists.T, block_masks, queries, keys, values, out_weight, out_grad)
    return pl.pallas_call(
        hand_on,
        out_shape=shapes,
        in_specs=[pl.BlockSpec(memory_space=pltpu.HBM)] * 4,
        out_specs=(pl.BlockSpec(memory_space=pltpu.HBM),) * 4,
        scratch_shapes=[dma((4,))],
    )(*results)


def solution(mesh):
    split = P("tm", "head")
    return jax.shard_map(
        functools.partial(local, mesh.shape["tm"], mesh.shape["head"]),
        mesh=mesh,
        in_specs=(split, split, split, P("head", None), split, P(), P("tm", None)),
        out_specs=(split, split, split, split),
        check_vma=False,
    )
```

```python
import functools
import math

import jax
import jax.numpy as jnp
from jax import lax
from jax.experimental import pallas as pl
from jax.experimental.pallas import tpu as pltpu
from jax.sharding import PartitionSpec as P

HD = 128
TILE = 128
GROUP = 4
LIST = 4
BLOCKS = 3
MESH = pl.DeviceIdType.MESH
NT = (((1,), (1,)), ((), ()))
TN = (((0,), (0,)), ((), ()))
LEAD = 2
AT_S2, AT_S3, AT_CMP, AT_RZ, AT_R1, AT_FIN = 1, 2, 3, 4, 5, 6
F32 = jnp.float32
LOG2E = math.log2(math.e)
BF16 = jnp.bfloat16


def kernel(
    n_tm, n_head, heads, rows,
    align, masks, q_hbm, k_hbm, v_hbm, w_hbm, og_hbm,
    mixed_hbm, qg_hbm, kg_hbm, vg_hbm,
    mixed_ref, qg_ref, kg_ref, vg_ref, q, w, og, ga_all, att, bias,
    kv, zprev, znext, s3buf,
    own, r3send, r3recv, to_prev, to_next, of_next, of_prev, r1send, r1recv,
    msend, mrecv, mown,
    out_sem, loc_sem, kv_sem, og_send, og_recv, m_send, m_recv,
    s1_send, s1_recv, z_send, z_recv, s3_send, s3_recv,
    r3_ssem, r3_rsem, zb_send, zb_recv, r1_ssem, r1_rsem,
):
    scale = 1.0 / math.sqrt(HD)
    me = lax.axis_index("tm")
    hd = lax.axis_index("head")
    cols = heads * HD
    planes = n_tm // GROUP
    plane = me // GROUP
    p = me % GROUP
    dx = 1 - 2 * (p % 2)
    dy = 2 - 4 * (p // 2)
    has_prev = plane > 0
    has_next = plane < planes - 1

    unit = 2 if heads % 2 == 0 else 1
    steps = heads // unit

    def sides(c):
        t = c % 2
        d1 = dx * (1 - t) + dy * t
        d2 = dy * (1 - t) + dx * t
        return d1, d2

    def flags(dest, r):
        prev = jnp.int32(0)
        nxt = jnp.int32(0)
        for s in range(LIST):
            a = align[s, dest]
            hit = jnp.logical_and(a >= 0, lax.rem(a + GROUP, GROUP) == r)
            pa = lax.div(a + GROUP, GROUP) - 1
            prev = jnp.where(jnp.logical_and(hit, pa < plane), 1, prev)
            nxt = jnp.where(jnp.logical_and(hit, pa > plane), 1, nxt)
        return prev, nxt

    def rcopy(src, dst, ss, rs, dev):
        return pltpu.make_async_remote_copy(
            src_ref=src, dst_ref=dst, send_sem=ss, recv_sem=rs,
            device_id=dev, device_id_type=MESH,
        )

    def s1_copy(c):
        d1, _ = sides(c)
        return rcopy(kv.at[c, 0], kv.at[c, 1], s1_send.at[c], s1_recv.at[c], {"tm": me + d1})

    def s3_copy(c):
        _, d2 = sides(c)
        return rcopy(
            s3buf.at[c], kv.at[c, pl.ds(2, 2)], s3_send.at[c], s3_recv.at[c], {"tm": me + d2}
        )

    def r3_copy(c):
        _, d2 = sides(c)
        return rcopy(r3send.at[c], r3recv.at[c], r3_ssem.at[c], r3_rsem.at[c], {"tm": me + d2})

    def r1_copy(c):
        d1, _ = sides(c)
        return rcopy(r1send.at[c], r1recv.at[c], r1_ssem.at[c], r1_rsem.at[c], {"tm": me + d1})

    def z_copies(c):
        d1, d2 = sides(c)
        out = []
        for j in range(2):
            r = p + (d1 if j else 0)
            up = jnp.logical_or(r > p, r > p + d2)
            down = jnp.logical_or(r < p, r < p + d2)
            out.append((
                jnp.logical_and(up, has_next),
                rcopy(kv.at[c, j], zprev.at[c, j], z_send.at[c, j], z_recv.at[c, j],
                      {"tm": me + GROUP}),
                jnp.logical_and(up, has_prev),
            ))
            out.append((
                jnp.logical_and(down, has_prev),
                rcopy(kv.at[c, j], znext.at[c, j], z_send.at[c, 2 + j], z_recv.at[c, 2 + j],
                      {"tm": me - GROUP}),
                jnp.logical_and(down, has_next),
            ))
        return out

    def zb_copies(c):
        d1, d2 = sides(c)
        out = []
        for j in range(2):
            r = p + (d1 if j else 0)
            up = jnp.logical_or(r > p, r > p + d2)
            down = jnp.logical_or(r < p, r < p + d2)
            out.append((
                jnp.logical_and(up, has_prev),
                rcopy(to_prev.at[c, j], of_next.at[c, j], zb_send.at[c, j], zb_recv.at[c, j],
                      {"tm": me - GROUP}),
                jnp.logical_and(up, has_next),
            ))
            out.append((
                jnp.logical_and(down, has_next),
                rcopy(to_next.at[c, j], of_prev.at[c, j], zb_send.at[c, 2 + j],
                      zb_recv.at[c, 2 + j], {"tm": me + GROUP}),
                jnp.logical_and(down, has_prev),
            ))
        return out

    def kv_copies(c):
        at = pl.ds(pl.multiple_of(c * HD, HD), HD)
        return (
            pltpu.make_async_copy(k_hbm.at[:, at], kv.at[c, 0, 0], kv_sem.at[c, 0]),
            pltpu.make_async_copy(v_hbm.at[:, at], kv.at[c, 0, 1], kv_sem.at[c, 1]),
        )

    def start_kv(c, carry):
        for copy in kv_copies(c):
            copy.start()
        return carry

    lax.fori_loop(0, heads, start_kv, 0)

    og_own = pl.ds(pl.multiple_of(hd * cols, HD), cols)
    local = (
        pltpu.make_async_copy(og_hbm, og.at[:, og_own], loc_sem.at[0]),
        pltpu.make_async_copy(q_hbm, q, loc_sem.at[1]),
        pltpu.make_async_copy(w_hbm, w, loc_sem.at[2]),
    )
    for copy in local:
        copy.start()

    barrier = pltpu.get_barrier_semaphore()
    pl.semaphore_signal(barrier, inc=1, device_id={"tm": me + dx}, device_id_type=MESH)
    pl.semaphore_signal(barrier, inc=1, device_id={"tm": me + dy}, device_id_type=MESH)

    @pl.when(has_prev)
    def _():
        pl.semaphore_signal(barrier, inc=1, device_id={"tm": me - GROUP}, device_id_type=MESH)

    @pl.when(has_next)
    def _():
        pl.semaphore_signal(barrier, inc=1, device_id={"tm": me + GROUP}, device_id_type=MESH)

    for k in range(1, n_head):
        pl.semaphore_signal(
            barrier, inc=1, device_id={"head": (hd + k) % n_head}, device_id_type=MESH
        )

    row = lax.broadcasted_iota(jnp.int32, (rows, GROUP * TILE), 0)
    col = lax.broadcasted_iota(jnp.int32, (rows, GROUP * TILE), 1)
    for t in range(2):
        d1, d2 = sides(t)
        residues = (p, p + d1, p + d2, p + d1 + d2)
        total = jnp.full((rows, GROUP * TILE), -1e30, F32)
        for i in range(rows // TILE):
            for j, r in enumerate(residues):
                live = jnp.float32(-1e30)
                for b in range(BLOCKS):
                    m = masks[i, b]
                    for s in range(LIST):
                        a = align[s, me]
                        hit = jnp.logical_and(m == s, lax.rem(a + GROUP, GROUP) == r)
                        live = jnp.where(hit, jnp.float32(0.0), live)
                here = jnp.logical_and(row // TILE == i, col // TILE == j)
                total = jnp.where(here, live, total)
        bias[t] = total

    near = 2 + (n_head - 1) + jnp.where(has_prev, 1, 0) + jnp.where(has_next, 1, 0)
    pl.semaphore_wait(barrier, near)

    def og_copy(k):
        return rcopy(
            og_hbm, og.at[:, og_own], og_send.at[k - 1], og_recv.at[k - 1],
            {"head": (hd + k) % n_head},
        )

    def og_arrival(k):
        src = (hd - k + n_head) % n_head
        return rcopy(
            og_hbm, og.at[:, pl.ds(pl.multiple_of(src * cols, HD), cols)],
            og_send.at[k - 1], og_recv.at[k - 1], {"head": (hd + k) % n_head},
        )

    def pick(c, j, prev, nxt):
        return jnp.where(prev > 0, zprev[c, j], jnp.where(nxt > 0, znext[c, j], kv[c, j]))

    def step(k, carry):
        def stage(skew, body):
            n = k - skew
            pl.when(jnp.logical_and(n >= 0, n < steps))(lambda: body([n * unit + u for u in range(unit)]))

        def s1(cs):
            for c in cs:
                for copy in kv_copies(c):
                    copy.wait()
                s1_copy(c).start()

        def s2(cs):
            for c in cs:
                s1_copy(c).wait_recv()
                for out, copy, _ in z_copies(c):
                    pl.when(out)(copy.start)

        def s3(cs):
            for c in cs:
                for _, copy, come in z_copies(c):
                    pl.when(come)(copy.wait_recv)
                d1, d2 = sides(c)
                for j in range(2):
                    prev, nxt = flags(me + d2, p + (d1 if j else 0))
                    s3buf[c, j] = pick(c, j, prev, nxt)
                s3_copy(c).start()

        def cmp(cs):
            for c in cs:
                s3_copy(c).wait_recv()
            at = [pl.ds(pl.multiple_of(c * HD, HD), HD) for c in cs]
            chosen = []
            for c in cs:
                prev, nxt = flags(me, p + sides(c)[0])
                chosen.append(pick(c, 1, prev, nxt))
            each = range(len(cs))
            kh = [
                jnp.concatenate([kv[cs[u], 0, 0], chosen[u][0], kv[cs[u], 2, 0], kv[cs[u], 3, 0]], 0)
                for u in each
            ]
            vh = [
                jnp.concatenate([kv[cs[u], 0, 1], chosen[u][1], kv[cs[u], 2, 1], kv[cs[u], 3, 1]], 0)
                for u in each
            ]
            qh = [q[:, at[u]] for u in each]
            ga = [ga_all[:, at[u]] for u in each]
            scores = [lax.dot_general(qh[u], kh[u], NT, preferred_element_type=F32) for u in each]
            gp = [lax.dot_general(ga[u], vh[u], NT, preferred_element_type=F32) for u in each]
            scores = [scores[u] * (scale * LOG2E) + bias[cs[u] % 2] for u in each]
            e = [jnp.exp2(x - jnp.max(x, -1, keepdims=True)) for x in scores]
            probs = [x * (1.0 / jnp.sum(x, -1, keepdims=True)) for x in e]
            weights = [x.astype(BF16) for x in probs]
            attended = [
                jnp.dot(weights[u], vh[u], preferred_element_type=F32).astype(BF16) for u in each
            ]
            vt = [lax.dot_general(weights[u], ga[u], TN, preferred_element_type=F32) for u in each]
            delta = [
                jnp.sum(ga[u].astype(F32) * attended[u].astype(F32), -1, keepdims=True) for u in each
            ]
            gs = [(probs[u] * (gp[u] - delta[u])).astype(BF16) for u in each]
            kt = [
                lax.dot_general(gs[u], qh[u], TN, preferred_element_type=F32) * scale for u in each
            ]
            for u in each:
                for j in range(2):
                    r3send[cs[u], j, 0] = kt[u][(2 + j) * TILE:(3 + j) * TILE].astype(BF16)
                    r3send[cs[u], j, 1] = vt[u][(2 + j) * TILE:(3 + j) * TILE].astype(BF16)
            for c in cs:
                r3_copy(c).start()
            for u in each:
                qg = jnp.dot(gs[u], kh[u], preferred_element_type=F32) * scale
                qg_ref[:, at[u]] = qg.astype(BF16)
                att[:, at[u]] = attended[u]
                for j in range(2):
                    own[cs[u], j, 0] = kt[u][j * TILE:(j + 1) * TILE]
                    own[cs[u], j, 1] = vt[u][j * TILE:(j + 1) * TILE]

        def rz(cs):
            for c in cs:
                d1, d2 = sides(c)
                r3_copy(c).wait_recv()
                for j in range(2):
                    r = p + (d1 if j else 0)
                    mp, mn = flags(me, r)
                    op, on = flags(me + d2, r)
                    mp, mn, op, on = (x.astype(F32) for x in (mp, mn, op, on))
                    mine = own[c, j]
                    other = r3recv[c, j].astype(F32)
                    to_prev[c, j] = (mine * mp + other * op).astype(BF16)
                    to_next[c, j] = (mine * mn + other * on).astype(BF16)
                    own[c, j] = mine * (1.0 - mp - mn) + other * (1.0 - op - on)
                for out, copy, _ in zb_copies(c):
                    pl.when(out)(copy.start)

        def r1(cs):
            for c in cs:
                copies = zb_copies(c)
                for _, copy, come in copies:
                    pl.when(come)(copy.wait_recv)
                sums = []
                for j in range(2):
                    total = own[c, j]
                    total = total + jnp.where(copies[2 * j][2], of_next[c, j].astype(F32), 0.0)
                    total = total + jnp.where(copies[2 * j + 1][2], of_prev[c, j].astype(F32), 0.0)
                    sums.append(total)
                r1send[c] = sums[1].astype(BF16)
                r1_copy(c).start()
                own[c, 0] = sums[0]

        def fin(cs):
            for c in cs:
                r1_copy(c).wait_recv()
                at = pl.ds(pl.multiple_of(c * HD, HD), HD)
                kg_ref[:, at] = (own[c, 0, 0] + r1recv[c, 0].astype(F32)).astype(BF16)
                vg_ref[:, at] = (own[c, 0, 1] + r1recv[c, 1].astype(F32)).astype(BF16)

        @pl.when(k == 0)
        def _():
            for kk in range(1, n_head):
                og_copy(kk).start()
            for n in range(lead):
                s1([n * unit + u for u in range(unit)])

        stage(-lead, s1)
        stage(AT_S2, s2)

        @pl.when(k == AT_S2)
        def _():
            for copy in local:
                copy.wait()
            for kk in range(1, n_head):
                og_arrival(kk).wait_recv()
            grads(0, blocks // 2)

        stage(AT_S3, s3)

        @pl.when(k == AT_S3)
        def _():
            grads(blocks // 2, blocks)

        stage(AT_CMP, cmp)

        @pl.when(k == steps + AT_CMP)
        def _():
            outs[1].start()
            for kk in range(1, n_head):
                mix(kk)

        stage(AT_RZ, rz)

        @pl.when(k == steps + AT_CMP)
        def _():
            mix(0)

        stage(AT_R1, r1)

        @pl.when(k == steps + AT_FIN - 1)
        def _():
            for kk in range(1, n_head):
                m_copy(kk).wait_recv()
            total = mown[...].astype(F32)
            for kk in range(1, n_head):
                total = total + mrecv[kk - 1].astype(F32)
            mixed_ref[...] = total.astype(BF16)
            outs[0].start()

        stage(AT_FIN, fin)
        return carry

    lead = min(LEAD, steps)
    block = 256 if cols % 256 == 0 else 128
    blocks = cols // block
    outs = tuple(
        pltpu.make_async_copy(src, dst, out_sem.at[i])
        for i, (src, dst) in enumerate((
            (mixed_ref, mixed_hbm), (qg_ref, qg_hbm), (kg_ref, kg_hbm), (vg_ref, vg_hbm),
        ))
    )

    def grads(first, last):
        def one(n, carry):
            at = pl.ds(pl.multiple_of(n * block, 128), block)
            ga = lax.dot_general(og[...], w[at, :], NT, preferred_element_type=F32)
            ga_all[:, at] = ga.astype(BF16)
            return carry

        lax.fori_loop(first, last, one, 0)

    def m_copy(k):
        return rcopy(
            msend.at[k - 1], mrecv.at[k - 1], m_send.at[k - 1], m_recv.at[k - 1],
            {"head": (hd + k) % n_head},
        )

    def mix(k):
        base = ((hd + k) % n_head) * cols
        out = msend.at[k - 1] if k else mown

        def one(n, carry):
            src = pl.ds(pl.multiple_of(base + n * block, 128), block)
            dst = pl.ds(pl.multiple_of(n * block, 128), block)
            part = jnp.dot(att[...], w[:, src], preferred_element_type=F32)
            out[:, dst] = part.astype(BF16)
            return carry

        lax.fori_loop(0, blocks, one, 0)
        if k:
            m_copy(k).start()

    lax.fori_loop(0, steps + AT_FIN, step, 0)

    outs[2].start()
    outs[3].start()

    def drain(c, carry):
        s1_copy(c).wait_send()
        s3_copy(c).wait_send()
        r3_copy(c).wait_send()
        r1_copy(c).wait_send()
        for out, copy, _ in z_copies(c) + zb_copies(c):
            pl.when(out)(copy.wait_send)
        return carry

    lax.fori_loop(0, heads, drain, 0)
    for k in range(1, n_head):
        og_copy(k).wait_send()
        m_copy(k).wait_send()
    for copy in outs:
        copy.wait()


def hand_on(*refs):
    come, go = refs[-2], refs[-1]
    n = (len(refs) - 2) // 3
    ins = [pltpu.make_async_copy(refs[i], refs[2 * n + i], come.at[i]) for i in range(n)]
    outs = [pltpu.make_async_copy(refs[2 * n + i], refs[n + i], go.at[i]) for i in range(n)]
    for copy in ins:
        copy.start()
    for i in range(n):
        ins[i].wait()
        outs[i].start()
    for copy in outs:
        copy.wait()


def local(n_tm, n_head, queries, keys, values, out_weight, out_grad, align_lists, block_masks):
    rows, cols = queries.shape
    heads = cols // HD
    width = out_weight.shape[1]
    others = max(n_head - 1, 1)
    pair = (2, TILE, HD)
    hbm = pl.BlockSpec(memory_space=pl.ANY)
    smem = pl.BlockSpec(memory_space=pltpu.SMEM)
    dma = pltpu.SemaphoreType.DMA
    V = pltpu.VMEM
    shapes = (
        jax.ShapeDtypeStruct((rows, cols), BF16),
        jax.ShapeDtypeStruct((rows, cols), BF16),
        jax.ShapeDtypeStruct(keys.shape, BF16),
        jax.ShapeDtypeStruct(keys.shape, BF16),
    )
    results = pl.pallas_call(
        functools.partial(kernel, n_tm, n_head, heads, rows),
        out_shape=shapes,
        in_specs=[smem, smem, hbm, hbm, hbm, hbm, hbm],
        out_specs=(hbm,) * 4,
        scratch_shapes=[
            V((rows, cols), BF16),
            V((rows, cols), BF16),
            V(keys.shape, BF16),
            V(keys.shape, BF16),
            V((rows, cols), BF16),
            V((cols, width), BF16),
            V((rows, width), BF16),
            V((rows, cols), BF16),
            V((rows, cols), BF16),
            V((2, rows, GROUP * TILE), F32),
            V((heads, 4) + pair, BF16),
            V((heads, 2) + pair, BF16),
            V((heads, 2) + pair, BF16),
            V((heads, 2) + pair, BF16),
            V((heads, 2) + pair, F32),
            V((heads, 2) + pair, BF16),
            V((heads, 2) + pair, BF16),
            V((heads, 2) + pair, BF16),
            V((heads, 2) + pair, BF16),
            V((heads, 2) + pair, BF16),
            V((heads, 2) + pair, BF16),
            V((heads,) + pair, BF16),
            V((heads,) + pair, BF16),
            V((others, rows, cols), BF16),
            V((others, rows, cols), BF16),
            V((rows, cols), BF16),
            dma((4,)),
            dma((3,)),
            dma((heads, 2)),
            dma((others,)),
            dma((others,)),
            dma((others,)),
            dma((others,)),
            dma((heads,)),
            dma((heads,)),
            dma((heads, 4)),
            dma((heads, 4)),
            dma((heads,)),
            dma((heads,)),
            dma((heads,)),
            dma((heads,)),
            dma((heads, 4)),
            dma((heads, 4)),
            dma((heads,)),
            dma((heads,)),
        ],
        compiler_params=pltpu.CompilerParams(
            collective_id=0, has_side_effects=True, vmem_limit_bytes=56 * 1024 * 1024
        ),
        cost_estimate=pl.CostEstimate(
            flops=4 * rows * cols * width + 12 * rows * GROUP * TILE * cols,
            bytes_accessed=2 * cols * width, transcendentals=rows * GROUP * TILE * heads,
        ),
    )(align_lists.T, block_masks, queries, keys, values, out_weight, out_grad)
    return pl.pallas_call(
        hand_on,
        out_shape=shapes,
        in_specs=[pl.BlockSpec(memory_space=pltpu.HBM)] * 4,
        out_specs=(pl.BlockSpec(memory_space=pltpu.HBM),) * 4,
        scratch_shapes=[V(x.shape, BF16) for x in shapes] + [dma((4,)), dma((4,))],
    )(*results)


def solution(mesh):
    split = P("tm", "head")
    return jax.shard_map(
        functools.partial(local, mesh.shape["tm"], mesh.shape["head"]),
        mesh=mesh,
        in_specs=(split, split, split, P("head", None), split, P(), P("tm", None)),
        out_specs=(split, split, split, split),
        check_vma=False,
    )
```

```python
import functools
import math

import jax
import jax.numpy as jnp
from jax import lax
from jax.experimental import pallas as pl
from jax.experimental.pallas import tpu as pltpu
from jax.sharding import PartitionSpec as P

HD = 128
TILE = 128
GROUP = 4
LIST = 4
BLOCKS = 3
MESH = pl.DeviceIdType.MESH
NT = (((1,), (1,)), ((), ()))
TN = (((0,), (0,)), ((), ()))
LEAD = 4
AT_S2, AT_S3, AT_CMP, AT_RZ, AT_R1, AT_FIN = 1, 2, 3, 4, 5, 6
F32 = jnp.float32
LOG2E = math.log2(math.e)
BF16 = jnp.bfloat16


def kernel(
    n_tm, n_head, heads, rows,
    align, masks, q_hbm, k_hbm, v_hbm, w_hbm, og_hbm,
    mixed_ref, qg_ref, kg_ref, vg_ref,
    q, w, og, ga_all, att, bias,
    kv, zprev, znext, s3buf,
    own, r3send, r3recv, to_prev, to_next, of_next, of_prev, r1send, r1recv,
    msend, mrecv, mown,
    loc_sem, kv_sem, og_send, og_recv, m_send, m_recv,
    s1_send, s1_recv, z_send, z_recv, s3_send, s3_recv,
    r3_ssem, r3_rsem, zb_send, zb_recv, r1_ssem, r1_rsem,
):
    scale = 1.0 / math.sqrt(HD)
    me = lax.axis_index("tm")
    hd = lax.axis_index("head")
    cols = heads * HD
    planes = n_tm // GROUP
    plane = me // GROUP
    p = me % GROUP
    dx = 1 - 2 * (p % 2)
    dy = 2 - 4 * (p // 2)
    has_prev = plane > 0
    has_next = plane < planes - 1

    unit = 2 if heads % 2 == 0 else 1
    steps = heads // unit

    def sides(c):
        t = c % 2
        d1 = dx * (1 - t) + dy * t
        d2 = dy * (1 - t) + dx * t
        return d1, d2

    def flags(dest, r):
        prev = jnp.int32(0)
        nxt = jnp.int32(0)
        for s in range(LIST):
            a = align[s, dest]
            hit = jnp.logical_and(a >= 0, lax.rem(a + GROUP, GROUP) == r)
            pa = lax.div(a + GROUP, GROUP) - 1
            prev = jnp.where(jnp.logical_and(hit, pa < plane), 1, prev)
            nxt = jnp.where(jnp.logical_and(hit, pa > plane), 1, nxt)
        return prev, nxt

    def rcopy(src, dst, ss, rs, dev):
        return pltpu.make_async_remote_copy(
            src_ref=src, dst_ref=dst, send_sem=ss, recv_sem=rs,
            device_id=dev, device_id_type=MESH,
        )

    def s1_copy(c):
        d1, _ = sides(c)
        return rcopy(kv.at[c, 0], kv.at[c, 1], s1_send.at[c], s1_recv.at[c], {"tm": me + d1})

    def s3_copy(c):
        _, d2 = sides(c)
        return rcopy(
            s3buf.at[c], kv.at[c, pl.ds(2, 2)], s3_send.at[c], s3_recv.at[c], {"tm": me + d2}
        )

    def r3_copy(c):
        _, d2 = sides(c)
        return rcopy(r3send.at[c], r3recv.at[c], r3_ssem.at[c], r3_rsem.at[c], {"tm": me + d2})

    def r1_copy(c):
        d1, _ = sides(c)
        return rcopy(r1send.at[c], r1recv.at[c], r1_ssem.at[c], r1_rsem.at[c], {"tm": me + d1})

    def z_copies(c):
        d1, d2 = sides(c)
        out = []
        for j in range(2):
            r = p + (d1 if j else 0)
            up = jnp.logical_or(r > p, r > p + d2)
            down = jnp.logical_or(r < p, r < p + d2)
            out.append((
                jnp.logical_and(up, has_next),
                rcopy(kv.at[c, j], zprev.at[c, j], z_send.at[c, j], z_recv.at[c, j],
                      {"tm": me + GROUP}),
                jnp.logical_and(up, has_prev),
            ))
            out.append((
                jnp.logical_and(down, has_prev),
                rcopy(kv.at[c, j], znext.at[c, j], z_send.at[c, 2 + j], z_recv.at[c, 2 + j],
                      {"tm": me - GROUP}),
                jnp.logical_and(down, has_next),
            ))
        return out

    def zb_copies(c):
        d1, d2 = sides(c)
        out = []
        for j in range(2):
            r = p + (d1 if j else 0)
            up = jnp.logical_or(r > p, r > p + d2)
            down = jnp.logical_or(r < p, r < p + d2)
            out.append((
                jnp.logical_and(up, has_prev),
                rcopy(to_prev.at[c, j], of_next.at[c, j], zb_send.at[c, j], zb_recv.at[c, j],
                      {"tm": me - GROUP}),
                jnp.logical_and(up, has_next),
            ))
            out.append((
                jnp.logical_and(down, has_next),
                rcopy(to_next.at[c, j], of_prev.at[c, j], zb_send.at[c, 2 + j],
                      zb_recv.at[c, 2 + j], {"tm": me + GROUP}),
                jnp.logical_and(down, has_prev),
            ))
        return out

    def kv_copies(c):
        at = pl.ds(pl.multiple_of(c * HD, HD), HD)
        return (
            pltpu.make_async_copy(k_hbm.at[:, at], kv.at[c, 0, 0], kv_sem.at[c, 0]),
            pltpu.make_async_copy(v_hbm.at[:, at], kv.at[c, 0, 1], kv_sem.at[c, 1]),
        )

    def start_kv(c, carry):
        for copy in kv_copies(c):
            copy.start()
        return carry

    lax.fori_loop(0, heads, start_kv, 0)

    og_own = pl.ds(pl.multiple_of(hd * cols, HD), cols)
    local = (
        pltpu.make_async_copy(og_hbm, og.at[:, og_own], loc_sem.at[0]),
        pltpu.make_async_copy(q_hbm, q, loc_sem.at[1]),
        pltpu.make_async_copy(w_hbm, w, loc_sem.at[2]),
    )
    for copy in local:
        copy.start()

    barrier = pltpu.get_barrier_semaphore()
    pl.semaphore_signal(barrier, inc=1, device_id={"tm": me + dx}, device_id_type=MESH)
    pl.semaphore_signal(barrier, inc=1, device_id={"tm": me + dy}, device_id_type=MESH)

    @pl.when(has_prev)
    def _():
        pl.semaphore_signal(barrier, inc=1, device_id={"tm": me - GROUP}, device_id_type=MESH)

    @pl.when(has_next)
    def _():
        pl.semaphore_signal(barrier, inc=1, device_id={"tm": me + GROUP}, device_id_type=MESH)

    for k in range(1, n_head):
        pl.semaphore_signal(
            barrier, inc=1, device_id={"head": (hd + k) % n_head}, device_id_type=MESH
        )

    near = 2 + (n_head - 1) + jnp.where(has_prev, 1, 0) + jnp.where(has_next, 1, 0)
    pl.semaphore_wait(barrier, near)

    def set_bias():
        row = lax.broadcasted_iota(jnp.int32, (rows, GROUP * TILE), 0)
        col = lax.broadcasted_iota(jnp.int32, (rows, GROUP * TILE), 1)
        for t in range(2):
            d1, d2 = sides(t)
            residues = (p, p + d1, p + d2, p + d1 + d2)
            total = jnp.full((rows, GROUP * TILE), -1e30, F32)
            for i in range(rows // TILE):
                for j, r in enumerate(residues):
                    live = jnp.float32(-1e30)
                    for b in range(BLOCKS):
                        m = masks[i, b]
                        for s in range(LIST):
                            a = align[s, me]
                            hit = jnp.logical_and(m == s, lax.rem(a + GROUP, GROUP) == r)
                            live = jnp.where(hit, jnp.float32(0.0), live)
                    here = jnp.logical_and(row // TILE == i, col // TILE == j)
                    total = jnp.where(here, live, total)
            bias[t] = total

    def og_copy(k):
        return rcopy(
            og_hbm, og.at[:, og_own], og_send.at[k - 1], og_recv.at[k - 1],
            {"head": (hd + k) % n_head},
        )

    def og_arrival(k):
        src = (hd - k + n_head) % n_head
        return rcopy(
            og_hbm, og.at[:, pl.ds(pl.multiple_of(src * cols, HD), cols)],
            og_send.at[k - 1], og_recv.at[k - 1], {"head": (hd + k) % n_head},
        )

    def pick(c, j, prev, nxt):
        return jnp.where(prev > 0, zprev[c, j], jnp.where(nxt > 0, znext[c, j], kv[c, j]))

    def step(k, carry):
        def stage(skew, body):
            n = k - skew
            pl.when(jnp.logical_and(n >= 0, n < steps))(lambda: body([n * unit + u for u in range(unit)]))

        def s1(cs):
            for c in cs:
                for copy in kv_copies(c):
                    copy.wait()
                s1_copy(c).start()

        def s2(cs):
            for c in cs:
                s1_copy(c).wait_recv()
                mine, theirs = z_copies(c)[:2], z_copies(c)[2:]
                for out, copy, _ in mine:
                    pl.when(jnp.logical_and(out, k > AT_S2))(copy.start)
                for out, copy, _ in theirs:
                    pl.when(out)(copy.start)

        def s3(cs):
            for c in cs:
                for _, copy, come in z_copies(c):
                    pl.when(come)(copy.wait_recv)
                d1, d2 = sides(c)
                for j in range(2):
                    prev, nxt = flags(me + d2, p + (d1 if j else 0))
                    s3buf[c, j] = pick(c, j, prev, nxt)
                s3_copy(c).start()

        def cmp(cs):
            for c in cs:
                s3_copy(c).wait_recv()
            at = [pl.ds(pl.multiple_of(c * HD, HD), HD) for c in cs]
            chosen = []
            for c in cs:
                prev, nxt = flags(me, p + sides(c)[0])
                chosen.append(pick(c, 1, prev, nxt))
            each = range(len(cs))
            kh = [
                jnp.concatenate([kv[cs[u], 0, 0], chosen[u][0], kv[cs[u], 2, 0], kv[cs[u], 3, 0]], 0)
                for u in each
            ]
            vh = [
                jnp.concatenate([kv[cs[u], 0, 1], chosen[u][1], kv[cs[u], 2, 1], kv[cs[u], 3, 1]], 0)
                for u in each
            ]
            qh = [q[:, at[u]] for u in each]
            ga = [ga_all[:, at[u]] for u in each]
            scores = [lax.dot_general(qh[u], kh[u], NT, preferred_element_type=F32) for u in each]
            gp = [lax.dot_general(ga[u], vh[u], NT, preferred_element_type=F32) for u in each]
            scores = [scores[u] * (scale * LOG2E) + bias[cs[u] % 2] for u in each]
            e = [jnp.exp2(x - jnp.max(x, -1, keepdims=True)) for x in scores]
            probs = [x * (1.0 / jnp.sum(x, -1, keepdims=True)) for x in e]
            weights = [x.astype(BF16) for x in probs]
            attended = [
                jnp.dot(weights[u], vh[u], preferred_element_type=F32).astype(BF16) for u in each
            ]
            vt = [lax.dot_general(weights[u], ga[u], TN, preferred_element_type=F32) for u in each]
            delta = [
                jnp.sum(ga[u].astype(F32) * attended[u].astype(F32), -1, keepdims=True) for u in each
            ]
            gs = [(probs[u] * (gp[u] - delta[u])).astype(BF16) for u in each]
            kt = [
                lax.dot_general(gs[u], qh[u], TN, preferred_element_type=F32) * scale for u in each
            ]
            for u in each:
                for j in range(2):
                    r3send[cs[u], j, 0] = kt[u][(2 + j) * TILE:(3 + j) * TILE].astype(BF16)
                    r3send[cs[u], j, 1] = vt[u][(2 + j) * TILE:(3 + j) * TILE].astype(BF16)
            for c in cs:
                r3_copy(c).start()
            for u in each:
                qg = jnp.dot(gs[u], kh[u], preferred_element_type=F32) * scale
                qg_ref[:, at[u]] = qg.astype(BF16)
                att[:, at[u]] = attended[u]
                for j in range(2):
                    own[cs[u], j, 0] = kt[u][j * TILE:(j + 1) * TILE]
                    own[cs[u], j, 1] = vt[u][j * TILE:(j + 1) * TILE]

        def rz(cs):
            for c in cs:
                d1, d2 = sides(c)
                r3_copy(c).wait_recv()
                for j in range(2):
                    r = p + (d1 if j else 0)
                    mp, mn = flags(me, r)
                    op, on = flags(me + d2, r)
                    mp, mn, op, on = (x.astype(F32) for x in (mp, mn, op, on))
                    mine = own[c, j]
                    other = r3recv[c, j].astype(F32)
                    to_prev[c, j] = (mine * mp + other * op).astype(BF16)
                    to_next[c, j] = (mine * mn + other * on).astype(BF16)
                    own[c, j] = mine * (1.0 - mp - mn) + other * (1.0 - op - on)
                for out, copy, _ in zb_copies(c)[2:]:
                    pl.when(out)(copy.start)
            for c in cs:
                for out, copy, _ in zb_copies(c)[:2]:
                    pl.when(out)(copy.start)

        def back(c, j):
            copies = zb_copies(c)[2 * j:2 * j + 2]
            for _, copy, come in copies:
                pl.when(come)(copy.wait_recv)
            total = own[c, j]
            total = total + jnp.where(copies[0][2], of_next[c, j].astype(F32), 0.0)
            return total + jnp.where(copies[1][2], of_prev[c, j].astype(F32), 0.0)

        def r1(cs):
            for c in cs:
                r1send[c] = back(c, 1).astype(BF16)
                r1_copy(c).start()

        def fin(cs):
            for c in cs:
                total = back(c, 0)
                r1_copy(c).wait_recv()
                at = pl.ds(pl.multiple_of(c * HD, HD), HD)
                kg_ref[:, at] = (total[0] + r1recv[c, 0].astype(F32)).astype(BF16)
                vg_ref[:, at] = (total[1] + r1recv[c, 1].astype(F32)).astype(BF16)

        @pl.when(k == 0)
        def _():
            for kk in range(1, n_head):
                og_copy(kk).start()
            for n in range(lead):
                s1([n * unit + u for u in range(unit)])
                if n == 0:
                    for u in range(unit):
                        for out, copy, _ in z_copies(u)[:2]:
                            pl.when(out)(copy.start)
            set_bias()

        stage(-lead, s1)
        stage(AT_S2, s2)

        @pl.when(k == AT_S2)
        def _():
            for copy in local:
                copy.wait()
            for kk in range(1, n_head):
                og_arrival(kk).wait_recv()
            grads(0, blocks // 2)

        stage(AT_S3, s3)

        @pl.when(k == AT_S3)
        def _():
            grads(blocks // 2, blocks)

        stage(AT_CMP, cmp)

        @pl.when(k == steps + AT_CMP)
        def _():
            for kk in range(1, n_head):
                mix(kk)

        stage(AT_RZ, rz)
        stage(AT_R1, r1)

        @pl.when(k == steps + AT_CMP)
        def _():
            mix(0)

        @pl.when(k == steps + AT_FIN - 1)
        def _():
            for kk in range(1, n_head):
                m_copy(kk).wait_recv()
            total = mown[...].astype(F32)
            for kk in range(1, n_head):
                total = total + mrecv[kk - 1].astype(F32)
            mixed_ref[...] = total.astype(BF16)

        stage(AT_FIN, fin)
        return carry

    lead = min(LEAD, steps)
    block = 256 if cols % 256 == 0 else 128
    blocks = cols // block
    def grads(first, last):
        def one(n, carry):
            at = pl.ds(pl.multiple_of(n * block, 128), block)
            ga = lax.dot_general(og[...], w[at, :], NT, preferred_element_type=F32)
            ga_all[:, at] = ga.astype(BF16)
            return carry

        lax.fori_loop(first, last, one, 0)

    def m_copy(k):
        return rcopy(
            msend.at[k - 1], mrecv.at[k - 1], m_send.at[k - 1], m_recv.at[k - 1],
            {"head": (hd + k) % n_head},
        )

    def mix(k):
        base = ((hd + k) % n_head) * cols
        out = msend.at[k - 1] if k else mown

        def one(n, carry):
            src = pl.ds(pl.multiple_of(base + n * block, 128), block)
            dst = pl.ds(pl.multiple_of(n * block, 128), block)
            part = jnp.dot(att[...], w[:, src], preferred_element_type=F32)
            out[:, dst] = part.astype(BF16)
            return carry

        lax.fori_loop(0, blocks, one, 0)
        if k:
            m_copy(k).start()

    lax.fori_loop(0, steps + AT_FIN, step, 0)

    def drain(c, carry):
        s1_copy(c).wait_send()
        s3_copy(c).wait_send()
        r3_copy(c).wait_send()
        r1_copy(c).wait_send()
        for out, copy, _ in z_copies(c) + zb_copies(c):
            pl.when(out)(copy.wait_send)
        return carry

    lax.fori_loop(0, heads, drain, 0)
    for k in range(1, n_head):
        og_copy(k).wait_send()
        m_copy(k).wait_send()


def hand_on(*refs):
    sems = refs[-1]
    n = len(refs) // 2
    copies = [pltpu.make_async_copy(refs[i], refs[n + i], sems.at[i]) for i in range(n)]
    for copy in copies:
        copy.start()
    for copy in copies:
        copy.wait()


def local(n_tm, n_head, queries, keys, values, out_weight, out_grad, align_lists, block_masks):
    rows, cols = queries.shape
    heads = cols // HD
    width = out_weight.shape[1]
    others = max(n_head - 1, 1)
    pair = (2, TILE, HD)
    hbm = pl.BlockSpec(memory_space=pltpu.HBM)
    vmem = pl.BlockSpec(memory_space=pltpu.VMEM)
    smem = pl.BlockSpec(memory_space=pltpu.SMEM)
    dma = pltpu.SemaphoreType.DMA
    V = pltpu.VMEM
    shapes = (
        jax.ShapeDtypeStruct((rows, cols), BF16),
        jax.ShapeDtypeStruct((rows, cols), BF16),
        jax.ShapeDtypeStruct(keys.shape, BF16),
        jax.ShapeDtypeStruct(keys.shape, BF16),
    )
    results = pl.pallas_call(
        functools.partial(kernel, n_tm, n_head, heads, rows),
        out_shape=tuple(V(x.shape, BF16) for x in shapes),
        in_specs=[smem, smem, hbm, hbm, hbm, hbm, hbm],
        out_specs=(vmem,) * 4,
        scratch_shapes=[
            V((rows, cols), BF16),
            V((cols, width), BF16),
            V((rows, width), BF16),
            V((rows, cols), BF16),
            V((rows, cols), BF16),
            V((2, rows, GROUP * TILE), F32),
            V((heads, 4) + pair, BF16),
            V((heads, 2) + pair, BF16),
            V((heads, 2) + pair, BF16),
            V((heads, 2) + pair, BF16),
            V((heads, 2) + pair, F32),
            V((heads, 2) + pair, BF16),
            V((heads, 2) + pair, BF16),
            V((heads, 2) + pair, BF16),
            V((heads, 2) + pair, BF16),
            V((heads, 2) + pair, BF16),
            V((heads, 2) + pair, BF16),
            V((heads,) + pair, BF16),
            V((heads,) + pair, BF16),
            V((others, rows, cols), BF16),
            V((others, rows, cols), BF16),
            V((rows, cols), BF16),
            dma((3,)),
            dma((heads, 2)),
            dma((others,)),
            dma((others,)),
            dma((others,)),
            dma((others,)),
            dma((heads,)),
            dma((heads,)),
            dma((heads, 4)),
            dma((heads, 4)),
            dma((heads,)),
            dma((heads,)),
            dma((heads,)),
            dma((heads,)),
            dma((heads, 4)),
            dma((heads, 4)),
            dma((heads,)),
            dma((heads,)),
        ],
        compiler_params=pltpu.CompilerParams(
            collective_id=0, has_side_effects=True, vmem_limit_bytes=59 * 1024 * 1024
        ),
        cost_estimate=pl.CostEstimate(
            flops=4 * rows * cols * width + 12 * rows * GROUP * TILE * cols,
            bytes_accessed=2 * cols * width, transcendentals=rows * GROUP * TILE * heads,
        ),
    )(align_lists.T, block_masks, queries, keys, values, out_weight, out_grad)
    return pl.pallas_call(
        hand_on,
        out_shape=shapes,
        in_specs=[vmem] * 4,
        out_specs=(pl.BlockSpec(memory_space=pltpu.HBM),) * 4,
        scratch_shapes=[dma((4,))],
    )(*results)


def solution(mesh):
    split = P("tm", "head")
    return jax.shard_map(
        functools.partial(local, mesh.shape["tm"], mesh.shape["head"]),
        mesh=mesh,
        in_specs=(split, split, split, P("head", None), split, P(), P("tm", None)),
        out_specs=(split, split, split, split),
        check_vma=False,
    )
```

```python
import functools
import math

import jax
import jax.numpy as jnp
from jax import lax
from jax.experimental import pallas as pl
from jax.experimental.pallas import tpu as pltpu
from jax.sharding import PartitionSpec as P

HD = 128
TILE = 128
GROUP = 4
LIST = 4
BLOCKS = 3
MESH = pl.DeviceIdType.MESH
NT = (((1,), (1,)), ((), ()))
TN = (((0,), (0,)), ((), ()))
LEAD = 4
AT_S2, AT_S3, AT_CMP, AT_RZ = 1, 2, 3, 4
F32 = jnp.float32
LOG2E = math.log2(math.e)
BF16 = jnp.bfloat16


def kernel(
    n_tm, n_head, heads, rows,
    align, masks, q_hbm, k_hbm, v_hbm, w_hbm, og_hbm,
    mixed_ref, qg_ref, kg_ref, vg_ref,
    q, w, og, ga_all, att, bias,
    kv, zprev, znext, s3buf,
    own, r3send, r3recv, to_prev, to_next, of_next, of_prev, r1send, r1recv,
    msend, mrecv, mown,
    loc_sem, kv_sem, og_send, og_recv, m_send, m_recv,
    s1_send, s1_recv, z_send, z_recv, s3_send, s3_recv,
    r3_ssem, r3_rsem, zb_send, zb_recv, r1_ssem, r1_rsem,
):
    scale = 1.0 / math.sqrt(HD)
    me = lax.axis_index("tm")
    hd = lax.axis_index("head")
    cols = heads * HD
    planes = n_tm // GROUP
    plane = me // GROUP
    p = me % GROUP
    dx = 1 - 2 * (p % 2)
    dy = 2 - 4 * (p // 2)
    has_prev = plane > 0
    has_next = plane < planes - 1

    unit = 2 if heads % 2 == 0 else 1
    steps = heads // unit

    def sides(c):
        t = c % 2
        d1 = dx * (1 - t) + dy * t
        d2 = dy * (1 - t) + dx * t
        return d1, d2

    def flags(dest, r):
        prev = jnp.int32(0)
        nxt = jnp.int32(0)
        for s in range(LIST):
            a = align[s, dest]
            hit = jnp.logical_and(a >= 0, lax.rem(a + GROUP, GROUP) == r)
            pa = lax.div(a + GROUP, GROUP) - 1
            prev = jnp.where(jnp.logical_and(hit, pa < plane), 1, prev)
            nxt = jnp.where(jnp.logical_and(hit, pa > plane), 1, nxt)
        return prev, nxt

    def rcopy(src, dst, ss, rs, dev):
        return pltpu.make_async_remote_copy(
            src_ref=src, dst_ref=dst, send_sem=ss, recv_sem=rs,
            device_id=dev, device_id_type=MESH,
        )

    def s1_copy(c):
        d1, _ = sides(c)
        return rcopy(kv.at[c, 0], kv.at[c, 1], s1_send.at[c], s1_recv.at[c], {"tm": me + d1})

    def s3_copy(c):
        _, d2 = sides(c)
        return rcopy(
            s3buf.at[c], kv.at[c, pl.ds(2, 2)], s3_send.at[c], s3_recv.at[c], {"tm": me + d2}
        )

    def r3_copy(c):
        _, d2 = sides(c)
        return rcopy(r3send.at[c], r3recv.at[c], r3_ssem.at[c], r3_rsem.at[c], {"tm": me + d2})

    def r1_copy(c):
        d1, _ = sides(c)
        return rcopy(r1send.at[c], r1recv.at[c], r1_ssem.at[c], r1_rsem.at[c], {"tm": me + d1})

    def z_copies(c):
        d1, d2 = sides(c)
        out = []
        for j in range(2):
            r = p + (d1 if j else 0)
            up = jnp.logical_or(r > p, r > p + d2)
            down = jnp.logical_or(r < p, r < p + d2)
            out.append((
                jnp.logical_and(up, has_next),
                rcopy(kv.at[c, j], zprev.at[c, j], z_send.at[c, j], z_recv.at[c, j],
                      {"tm": me + GROUP}),
                jnp.logical_and(up, has_prev),
            ))
            out.append((
                jnp.logical_and(down, has_prev),
                rcopy(kv.at[c, j], znext.at[c, j], z_send.at[c, 2 + j], z_recv.at[c, 2 + j],
                      {"tm": me - GROUP}),
                jnp.logical_and(down, has_next),
            ))
        return out

    def zb_copies(c):
        d1, d2 = sides(c)
        out = []
        for j in range(2):
            r = p + (d1 if j else 0)
            up = jnp.logical_or(r > p, r > p + d2)
            down = jnp.logical_or(r < p, r < p + d2)
            out.append((
                jnp.logical_and(up, has_prev),
                rcopy(to_prev.at[c, j], of_next.at[c, j], zb_send.at[c, j], zb_recv.at[c, j],
                      {"tm": me - GROUP}),
                jnp.logical_and(up, has_next),
            ))
            out.append((
                jnp.logical_and(down, has_next),
                rcopy(to_next.at[c, j], of_prev.at[c, j], zb_send.at[c, 2 + j],
                      zb_recv.at[c, 2 + j], {"tm": me + GROUP}),
                jnp.logical_and(down, has_prev),
            ))
        return out

    def kv_copies(c):
        at = pl.ds(pl.multiple_of(c * HD, HD), HD)
        return (
            pltpu.make_async_copy(k_hbm.at[:, at], kv.at[c, 0, 0], kv_sem.at[c, 0]),
            pltpu.make_async_copy(v_hbm.at[:, at], kv.at[c, 0, 1], kv_sem.at[c, 1]),
        )

    def start_kv(c, carry):
        for copy in kv_copies(c):
            copy.start()
        return carry

    lax.fori_loop(0, heads, start_kv, 0)

    og_own = pl.ds(pl.multiple_of(hd * cols, HD), cols)
    local = (
        pltpu.make_async_copy(og_hbm, og.at[:, og_own], loc_sem.at[0]),
        pltpu.make_async_copy(q_hbm, q, loc_sem.at[1]),
        pltpu.make_async_copy(w_hbm, w, loc_sem.at[2]),
    )
    for copy in local:
        copy.start()

    barrier = pltpu.get_barrier_semaphore()
    pl.semaphore_signal(barrier, inc=1, device_id={"tm": me + dx}, device_id_type=MESH)
    pl.semaphore_signal(barrier, inc=1, device_id={"tm": me + dy}, device_id_type=MESH)

    @pl.when(has_prev)
    def _():
        pl.semaphore_signal(barrier, inc=1, device_id={"tm": me - GROUP}, device_id_type=MESH)

    @pl.when(has_next)
    def _():
        pl.semaphore_signal(barrier, inc=1, device_id={"tm": me + GROUP}, device_id_type=MESH)

    for k in range(1, n_head):
        pl.semaphore_signal(
            barrier, inc=1, device_id={"head": (hd + k) % n_head}, device_id_type=MESH
        )

    near = 2 + (n_head - 1) + jnp.where(has_prev, 1, 0) + jnp.where(has_next, 1, 0)
    pl.semaphore_wait(barrier, near)

    def set_bias():
        row = lax.broadcasted_iota(jnp.int32, (rows, GROUP * TILE), 0)
        col = lax.broadcasted_iota(jnp.int32, (rows, GROUP * TILE), 1)
        for t in range(2):
            d1, d2 = sides(t)
            residues = (p, p + d1, p + d2, p + d1 + d2)
            total = jnp.full((rows, GROUP * TILE), -1e30, F32)
            for i in range(rows // TILE):
                for j, r in enumerate(residues):
                    live = jnp.float32(-1e30)
                    for b in range(BLOCKS):
                        m = masks[i, b]
                        for s in range(LIST):
                            a = align[s, me]
                            hit = jnp.logical_and(m == s, lax.rem(a + GROUP, GROUP) == r)
                            live = jnp.where(hit, jnp.float32(0.0), live)
                    here = jnp.logical_and(row // TILE == i, col // TILE == j)
                    total = jnp.where(here, live, total)
            bias[t] = total

    def og_copy(k):
        return rcopy(
            og_hbm, og.at[:, og_own], og_send.at[k - 1], og_recv.at[k - 1],
            {"head": (hd + k) % n_head},
        )

    def og_arrival(k):
        src = (hd - k + n_head) % n_head
        return rcopy(
            og_hbm, og.at[:, pl.ds(pl.multiple_of(src * cols, HD), cols)],
            og_send.at[k - 1], og_recv.at[k - 1], {"head": (hd + k) % n_head},
        )

    def pick(c, j, prev, nxt):
        return jnp.where(prev > 0, zprev[c, j], jnp.where(nxt > 0, znext[c, j], kv[c, j]))

    def back(c, j):
        copies = zb_copies(c)[2 * j:2 * j + 2]
        for _, copy, come in copies:
            pl.when(come)(copy.wait_recv)
        total = own[c, j]
        total = total + jnp.where(copies[0][2], of_next[c, j].astype(F32), 0.0)
        return total + jnp.where(copies[1][2], of_prev[c, j].astype(F32), 0.0)

    def r1(cs):
        for c in cs:
            r1send[c] = back(c, 1).astype(BF16)
            r1_copy(c).start()

    def fin(cs):
        for c in cs:
            total = back(c, 0)
            r1_copy(c).wait_recv()
            at = pl.ds(pl.multiple_of(c * HD, HD), HD)
            kg_ref[:, at] = (total[0] + r1recv[c, 0].astype(F32)).astype(BF16)
            vg_ref[:, at] = (total[1] + r1recv[c, 1].astype(F32)).astype(BF16)

    def pair(n):
        return [n * unit + u for u in range(unit)]

    def each_pair(first, last, body):
        def one(n, carry):
            body(pair(n))
            return carry

        lax.fori_loop(first, last, one, 0)

    def step(k, carry):
        def stage(skew, body):
            n = k - skew
            pl.when(jnp.logical_and(n >= 0, n < steps))(lambda: body(pair(n)))

        def s1(cs):
            for c in cs:
                for copy in kv_copies(c):
                    copy.wait()
                s1_copy(c).start()

        def s2(cs):
            for c in cs:
                s1_copy(c).wait_recv()
                mine, theirs = z_copies(c)[:2], z_copies(c)[2:]
                for out, copy, _ in mine:
                    pl.when(jnp.logical_and(out, k > AT_S2))(copy.start)
                for out, copy, _ in theirs:
                    pl.when(out)(copy.start)

        def s3(cs):
            for c in cs:
                for _, copy, come in z_copies(c):
                    pl.when(come)(copy.wait_recv)
                d1, d2 = sides(c)
                for j in range(2):
                    prev, nxt = flags(me + d2, p + (d1 if j else 0))
                    s3buf[c, j] = pick(c, j, prev, nxt)
                s3_copy(c).start()

        def cmp(cs):
            for c in cs:
                s3_copy(c).wait_recv()
            at = [pl.ds(pl.multiple_of(c * HD, HD), HD) for c in cs]
            chosen = []
            for c in cs:
                prev, nxt = flags(me, p + sides(c)[0])
                chosen.append(pick(c, 1, prev, nxt))
            each = range(len(cs))
            kh = [
                jnp.concatenate([kv[cs[u], 0, 0], chosen[u][0], kv[cs[u], 2, 0], kv[cs[u], 3, 0]], 0)
                for u in each
            ]
            vh = [
                jnp.concatenate([kv[cs[u], 0, 1], chosen[u][1], kv[cs[u], 2, 1], kv[cs[u], 3, 1]], 0)
                for u in each
            ]
            qh = [q[:, at[u]] for u in each]
            ga = [ga_all[:, at[u]] for u in each]
            scores = [lax.dot_general(qh[u], kh[u], NT, preferred_element_type=F32) for u in each]
            gp = [lax.dot_general(ga[u], vh[u], NT, preferred_element_type=F32) for u in each]
            scores = [scores[u] * (scale * LOG2E) + bias[cs[u] % 2] for u in each]
            e = [jnp.exp2(x - jnp.max(x, -1, keepdims=True)) for x in scores]
            probs = [x * (1.0 / jnp.sum(x, -1, keepdims=True)) for x in e]
            weights = [x.astype(BF16) for x in probs]
            attended = [
                jnp.dot(weights[u], vh[u], preferred_element_type=F32).astype(BF16) for u in each
            ]
            vt = [lax.dot_general(weights[u], ga[u], TN, preferred_element_type=F32) for u in each]
            delta = [
                jnp.sum(ga[u].astype(F32) * attended[u].astype(F32), -1, keepdims=True) for u in each
            ]
            gs = [(probs[u] * (gp[u] - delta[u])).astype(BF16) for u in each]
            kt = [
                lax.dot_general(gs[u], qh[u], TN, preferred_element_type=F32) * scale for u in each
            ]
            for u in each:
                for j in range(2):
                    r3send[cs[u], j, 0] = kt[u][(2 + j) * TILE:(3 + j) * TILE].astype(BF16)
                    r3send[cs[u], j, 1] = vt[u][(2 + j) * TILE:(3 + j) * TILE].astype(BF16)
            for c in cs:
                r3_copy(c).start()
            for u in each:
                qg = jnp.dot(gs[u], kh[u], preferred_element_type=F32) * scale
                qg_ref[:, at[u]] = qg.astype(BF16)
                att[:, at[u]] = attended[u]
                for j in range(2):
                    own[cs[u], j, 0] = kt[u][j * TILE:(j + 1) * TILE]
                    own[cs[u], j, 1] = vt[u][j * TILE:(j + 1) * TILE]

        def rz(cs):
            for c in cs:
                d1, d2 = sides(c)
                r3_copy(c).wait_recv()
                for j in range(2):
                    r = p + (d1 if j else 0)
                    mp, mn = flags(me, r)
                    op, on = flags(me + d2, r)
                    mp, mn, op, on = (x.astype(F32) for x in (mp, mn, op, on))
                    mine = own[c, j]
                    other = r3recv[c, j].astype(F32)
                    to_prev[c, j] = (mine * mp + other * op).astype(BF16)
                    to_next[c, j] = (mine * mn + other * on).astype(BF16)
                    own[c, j] = mine * (1.0 - mp - mn) + other * (1.0 - op - on)
                for out, copy, _ in zb_copies(c)[2:]:
                    pl.when(out)(copy.start)
            for c in cs:
                for out, copy, _ in zb_copies(c)[:2]:
                    pl.when(out)(copy.start)

        @pl.when(k == 0)
        def _():
            for kk in range(1, n_head):
                og_copy(kk).start()
            for n in range(lead):
                s1(pair(n))
                if n == 0:
                    for u in range(unit):
                        for out, copy, _ in z_copies(u)[:2]:
                            pl.when(out)(copy.start)
            set_bias()

        stage(-lead, s1)
        stage(AT_S2, s2)

        @pl.when(k == AT_S2)
        def _():
            for copy in local:
                copy.wait()
            for kk in range(1, n_head):
                og_arrival(kk).wait_recv()
            grads(0, blocks // 2)

        stage(AT_S3, s3)

        @pl.when(k == AT_S3)
        def _():
            grads(blocks // 2, blocks)

        stage(AT_CMP, cmp)

        @pl.when(k == steps + AT_CMP)
        def _():
            for kk in range(1, n_head):
                mix(kk)
            each_pair(0, steps - 2, r1)

        stage(AT_RZ, rz)
        return carry

    lead = min(LEAD, steps)
    block = 256 if cols % 256 == 0 else 128
    blocks = cols // block
    def grads(first, last):
        def one(n, carry):
            at = pl.ds(pl.multiple_of(n * block, 128), block)
            ga = lax.dot_general(og[...], w[at, :], NT, preferred_element_type=F32)
            ga_all[:, at] = ga.astype(BF16)
            return carry

        lax.fori_loop(first, last, one, 0)

    def m_copy(k):
        return rcopy(
            msend.at[k - 1], mrecv.at[k - 1], m_send.at[k - 1], m_recv.at[k - 1],
            {"head": (hd + k) % n_head},
        )

    def mix(k):
        base = ((hd + k) % n_head) * cols
        out = msend.at[k - 1] if k else mown

        def one(n, carry):
            src = pl.ds(pl.multiple_of(base + n * block, 128), block)
            dst = pl.ds(pl.multiple_of(n * block, 128), block)
            part = jnp.dot(att[...], w[:, src], preferred_element_type=F32)
            out[:, dst] = part.astype(BF16)
            return carry

        lax.fori_loop(0, blocks, one, 0)
        if k:
            m_copy(k).start()

    lax.fori_loop(0, steps + AT_RZ, step, 0)
    r1(pair(steps - 2))
    mix(0)
    r1(pair(steps - 1))
    for kk in range(1, n_head):
        m_copy(kk).wait_recv()
    total = mown[...].astype(F32)
    for kk in range(1, n_head):
        total = total + mrecv[kk - 1].astype(F32)
    mixed_ref[...] = total.astype(BF16)
    each_pair(0, steps, fin)

    def drain(c, carry):
        s1_copy(c).wait_send()
        s3_copy(c).wait_send()
        r3_copy(c).wait_send()
        r1_copy(c).wait_send()
        for out, copy, _ in z_copies(c) + zb_copies(c):
            pl.when(out)(copy.wait_send)
        return carry

    lax.fori_loop(0, heads, drain, 0)
    for k in range(1, n_head):
        og_copy(k).wait_send()
        m_copy(k).wait_send()


def hand_on(*refs):
    sems = refs[-1]
    n = len(refs) // 2
    copies = [pltpu.make_async_copy(refs[i], refs[n + i], sems.at[i]) for i in range(n)]
    for copy in copies:
        copy.start()
    for copy in copies:
        copy.wait()


def local(n_tm, n_head, queries, keys, values, out_weight, out_grad, align_lists, block_masks):
    rows, cols = queries.shape
    heads = cols // HD
    width = out_weight.shape[1]
    others = max(n_head - 1, 1)
    pair = (2, TILE, HD)
    hbm = pl.BlockSpec(memory_space=pltpu.HBM)
    vmem = pl.BlockSpec(memory_space=pltpu.VMEM)
    smem = pl.BlockSpec(memory_space=pltpu.SMEM)
    dma = pltpu.SemaphoreType.DMA
    V = pltpu.VMEM
    shapes = (
        jax.ShapeDtypeStruct((rows, cols), BF16),
        jax.ShapeDtypeStruct((rows, cols), BF16),
        jax.ShapeDtypeStruct(keys.shape, BF16),
        jax.ShapeDtypeStruct(keys.shape, BF16),
    )
    results = pl.pallas_call(
        functools.partial(kernel, n_tm, n_head, heads, rows),
        out_shape=tuple(V(x.shape, BF16) for x in shapes),
        in_specs=[smem, smem, hbm, hbm, hbm, hbm, hbm],
        out_specs=(vmem,) * 4,
        scratch_shapes=[
            V((rows, cols), BF16),
            V((cols, width), BF16),
            V((rows, width), BF16),
            V((rows, cols), BF16),
            V((rows, cols), BF16),
            V((2, rows, GROUP * TILE), F32),
            V((heads, 4) + pair, BF16),
            V((heads, 2) + pair, BF16),
            V((heads, 2) + pair, BF16),
            V((heads, 2) + pair, BF16),
            V((heads, 2) + pair, F32),
            V((heads, 2) + pair, BF16),
            V((heads, 2) + pair, BF16),
            V((heads, 2) + pair, BF16),
            V((heads, 2) + pair, BF16),
            V((heads, 2) + pair, BF16),
            V((heads, 2) + pair, BF16),
            V((heads,) + pair, BF16),
            V((heads,) + pair, BF16),
            V((others, rows, cols), BF16),
            V((others, rows, cols), BF16),
            V((rows, cols), BF16),
            dma((3,)),
            dma((heads, 2)),
            dma((others,)),
            dma((others,)),
            dma((others,)),
            dma((others,)),
            dma((heads,)),
            dma((heads,)),
            dma((heads, 4)),
            dma((heads, 4)),
            dma((heads,)),
            dma((heads,)),
            dma((heads,)),
            dma((heads,)),
            dma((heads, 4)),
            dma((heads, 4)),
            dma((heads,)),
            dma((heads,)),
        ],
        compiler_params=pltpu.CompilerParams(
            collective_id=0, has_side_effects=True, vmem_limit_bytes=59 * 1024 * 1024
        ),
        cost_estimate=pl.CostEstimate(
            flops=4 * rows * cols * width + 12 * rows * GROUP * TILE * cols,
            bytes_accessed=2 * cols * width, transcendentals=rows * GROUP * TILE * heads,
        ),
    )(align_lists.T, block_masks, queries, keys, values, out_weight, out_grad)
    return pl.pallas_call(
        hand_on,
        out_shape=shapes,
        in_specs=[vmem] * 4,
        out_specs=(pl.BlockSpec(memory_space=pltpu.HBM),) * 4,
        scratch_shapes=[dma((4,))],
        compiler_params=pltpu.CompilerParams(vmem_limit_bytes=1024 * 1024),
    )(*results)


def solution(mesh):
    split = P("tm", "head")
    return jax.shard_map(
        functools.partial(local, mesh.shape["tm"], mesh.shape["head"]),
        mesh=mesh,
        in_specs=(split, split, split, P("head", None), split, P(), P("tm", None)),
        out_specs=(split, split, split, split),
        check_vma=False,
    )
```

```python
import functools
import math

import jax
import jax.numpy as jnp
from jax import lax
from jax.experimental import pallas as pl
from jax.experimental.pallas import tpu as pltpu
from jax.sharding import PartitionSpec as P

HD = 128
TILE = 128
GROUP = 4
LIST = 4
BLOCKS = 3
MESH = pl.DeviceIdType.MESH
NT = (((1,), (1,)), ((), ()))
TN = (((0,), (0,)), ((), ()))
LEAD = 2
AT_S2, AT_S3, AT_CMP, AT_RZ = 1, 2, 3, 4
F32 = jnp.float32
LOG2E = math.log2(math.e)
BF16 = jnp.bfloat16


def kernel(
    n_tm, n_head, heads, rows,
    align, masks, q_hbm, k_hbm, v_hbm, w_hbm, og_hbm,
    mixed_ref, qg_ref, kg_ref, vg_ref,
    q, w, og, ga_all, att, bias,
    kv, zprev, znext, s3buf,
    own, r3send, r3recv, to_prev, to_next, of_next, of_prev, r1send, r1recv,
    msend, mrecv, mown,
    loc_sem, kv_sem, og_send, og_recv, m_send, m_recv,
    s1_send, s1_recv, z_send, z_recv, s3_send, s3_recv,
    r3_ssem, r3_rsem, zb_send, zb_recv, r1_ssem, r1_rsem,
):
    scale = 1.0 / math.sqrt(HD)
    me = lax.axis_index("tm")
    hd = lax.axis_index("head")
    cols = heads * HD
    planes = n_tm // GROUP
    plane = me // GROUP
    p = me % GROUP
    dx = 1 - 2 * (p % 2)
    dy = 2 - 4 * (p // 2)
    has_prev = plane > 0
    has_next = plane < planes - 1

    unit = 2 if heads % 2 == 0 else 1
    steps = heads // unit

    def sides(c):
        t = c % 2
        d1 = dx * (1 - t) + dy * t
        d2 = dy * (1 - t) + dx * t
        return d1, d2

    def flags(dest, r):
        prev = jnp.int32(0)
        nxt = jnp.int32(0)
        for s in range(LIST):
            a = align[s, dest]
            hit = jnp.logical_and(a >= 0, lax.rem(a + GROUP, GROUP) == r)
            pa = lax.div(a + GROUP, GROUP) - 1
            prev = jnp.where(jnp.logical_and(hit, pa < plane), 1, prev)
            nxt = jnp.where(jnp.logical_and(hit, pa > plane), 1, nxt)
        return prev, nxt

    def rcopy(src, dst, ss, rs, dev):
        return pltpu.make_async_remote_copy(
            src_ref=src, dst_ref=dst, send_sem=ss, recv_sem=rs,
            device_id=dev, device_id_type=MESH,
        )

    def s1_copy(c):
        d1, _ = sides(c)
        return rcopy(kv.at[c, 0], kv.at[c, 1], s1_send.at[c], s1_recv.at[c], {"tm": me + d1})

    def s3_copy(c):
        _, d2 = sides(c)
        return rcopy(
            s3buf.at[c], kv.at[c, pl.ds(2, 2)], s3_send.at[c], s3_recv.at[c], {"tm": me + d2}
        )

    def r3_copy(c):
        _, d2 = sides(c)
        return rcopy(r3send.at[c], r3recv.at[c], r3_ssem.at[c], r3_rsem.at[c], {"tm": me + d2})

    def r1_copy(c):
        d1, _ = sides(c)
        return rcopy(r1send.at[c], r1recv.at[c], r1_ssem.at[c], r1_rsem.at[c], {"tm": me + d1})

    def z_copies(c):
        d1, d2 = sides(c)
        out = []
        for j in range(2):
            r = p + (d1 if j else 0)
            up = jnp.logical_or(r > p, r > p + d2)
            down = jnp.logical_or(r < p, r < p + d2)
            out.append((
                jnp.logical_and(up, has_next),
                rcopy(kv.at[c, j], zprev.at[c, j], z_send.at[c, j], z_recv.at[c, j],
                      {"tm": me + GROUP}),
                jnp.logical_and(up, has_prev),
            ))
            out.append((
                jnp.logical_and(down, has_prev),
                rcopy(kv.at[c, j], znext.at[c, j], z_send.at[c, 2 + j], z_recv.at[c, 2 + j],
                      {"tm": me - GROUP}),
                jnp.logical_and(down, has_next),
            ))
        return out

    def zb_copies(c):
        d1, d2 = sides(c)
        out = []
        for j in range(2):
            r = p + (d1 if j else 0)
            up = jnp.logical_or(r > p, r > p + d2)
            down = jnp.logical_or(r < p, r < p + d2)
            out.append((
                jnp.logical_and(up, has_prev),
                rcopy(to_prev.at[c, j], of_next.at[c, j], zb_send.at[c, j], zb_recv.at[c, j],
                      {"tm": me - GROUP}),
                jnp.logical_and(up, has_next),
            ))
            out.append((
                jnp.logical_and(down, has_next),
                rcopy(to_next.at[c, j], of_prev.at[c, j], zb_send.at[c, 2 + j],
                      zb_recv.at[c, 2 + j], {"tm": me + GROUP}),
                jnp.logical_and(down, has_prev),
            ))
        return out

    def kv_copies(c):
        at = pl.ds(pl.multiple_of(c * HD, HD), HD)
        return (
            pltpu.make_async_copy(k_hbm.at[:, at], kv.at[c, 0, 0], kv_sem.at[c, 0]),
            pltpu.make_async_copy(v_hbm.at[:, at], kv.at[c, 0, 1], kv_sem.at[c, 1]),
        )

    def start_kv(c, carry):
        for copy in kv_copies(c):
            copy.start()
        return carry

    lax.fori_loop(0, heads, start_kv, 0)

    og_own = pl.ds(pl.multiple_of(hd * cols, HD), cols)
    local = (
        pltpu.make_async_copy(og_hbm, og.at[:, og_own], loc_sem.at[0]),
        pltpu.make_async_copy(q_hbm, q, loc_sem.at[1]),
        pltpu.make_async_copy(w_hbm, w, loc_sem.at[2]),
    )
    for copy in local:
        copy.start()

    barrier = pltpu.get_barrier_semaphore()
    pl.semaphore_signal(barrier, inc=1, device_id={"tm": me + dx}, device_id_type=MESH)
    pl.semaphore_signal(barrier, inc=1, device_id={"tm": me + dy}, device_id_type=MESH)

    @pl.when(has_prev)
    def _():
        pl.semaphore_signal(barrier, inc=1, device_id={"tm": me - GROUP}, device_id_type=MESH)

    @pl.when(has_next)
    def _():
        pl.semaphore_signal(barrier, inc=1, device_id={"tm": me + GROUP}, device_id_type=MESH)

    for k in range(1, n_head):
        pl.semaphore_signal(
            barrier, inc=1, device_id={"head": (hd + k) % n_head}, device_id_type=MESH
        )

    near = 2 + (n_head - 1) + jnp.where(has_prev, 1, 0) + jnp.where(has_next, 1, 0)
    pl.semaphore_wait(barrier, near)

    def set_bias():
        row = lax.broadcasted_iota(jnp.int32, (rows, GROUP * TILE), 0)
        col = lax.broadcasted_iota(jnp.int32, (rows, GROUP * TILE), 1)
        for t in range(2):
            d1, d2 = sides(t)
            residues = (p, p + d1, p + d2, p + d1 + d2)
            total = jnp.full((rows, GROUP * TILE), -1e30, F32)
            for i in range(rows // TILE):
                for j, r in enumerate(residues):
                    live = jnp.float32(-1e30)
                    for b in range(BLOCKS):
                        m = masks[i, b]
                        for s in range(LIST):
                            a = align[s, me]
                            hit = jnp.logical_and(m == s, lax.rem(a + GROUP, GROUP) == r)
                            live = jnp.where(hit, jnp.float32(0.0), live)
                    here = jnp.logical_and(row // TILE == i, col // TILE == j)
                    total = jnp.where(here, live, total)
            bias[t] = total

    def og_copy(k):
        return rcopy(
            og_hbm, og.at[:, og_own], og_send.at[k - 1], og_recv.at[k - 1],
            {"head": (hd + k) % n_head},
        )

    def og_arrival(k):
        src = (hd - k + n_head) % n_head
        return rcopy(
            og_hbm, og.at[:, pl.ds(pl.multiple_of(src * cols, HD), cols)],
            og_send.at[k - 1], og_recv.at[k - 1], {"head": (hd + k) % n_head},
        )

    def pick(c, j, prev, nxt):
        return jnp.where(prev > 0, zprev[c, j], jnp.where(nxt > 0, znext[c, j], kv[c, j]))

    hold = steps + 1
    early = max(steps - 4, 0)

    def zb_own(cs):
        for c in cs:
            for out, copy, _ in zb_copies(c)[:2]:
                pl.when(out)(copy.start)

    def back(c, j):
        copies = zb_copies(c)[2 * j:2 * j + 2]
        for _, copy, come in copies:
            pl.when(come)(copy.wait_recv)
        total = own[c, j]
        total = total + jnp.where(copies[0][2], of_next[c, j].astype(F32), 0.0)
        return total + jnp.where(copies[1][2], of_prev[c, j].astype(F32), 0.0)

    def r1(cs):
        for c in cs:
            r1send[c] = back(c, 1).astype(BF16)
            r1_copy(c).start()

    def fin(cs):
        for c in cs:
            total = back(c, 0)
            r1_copy(c).wait_recv()
            at = pl.ds(pl.multiple_of(c * HD, HD), HD)
            kg_ref[:, at] = (total[0] + r1recv[c, 0].astype(F32)).astype(BF16)
            vg_ref[:, at] = (total[1] + r1recv[c, 1].astype(F32)).astype(BF16)

    def pair(n):
        return [n * unit + u for u in range(unit)]

    def each_pair(first, last, body):
        def one(n, carry):
            body(pair(n))
            return carry

        lax.fori_loop(first, last, one, 0)

    def step(k, carry):
        def stage(skew, body):
            n = k - skew
            pl.when(jnp.logical_and(n >= 0, n < steps))(lambda: body(pair(n)))

        def s1(cs):
            for c in cs:
                for copy in kv_copies(c):
                    copy.wait()
                s1_copy(c).start()

        def s2(cs):
            for c in cs:
                s1_copy(c).wait_recv()
                mine, theirs = z_copies(c)[:2], z_copies(c)[2:]
                for out, copy, _ in mine:
                    pl.when(jnp.logical_and(out, k > AT_S2))(copy.start)
                for out, copy, _ in theirs:
                    pl.when(out)(copy.start)

        def s3(cs):
            for c in cs:
                for _, copy, come in z_copies(c):
                    pl.when(come)(copy.wait_recv)
                d1, d2 = sides(c)
                for j in range(2):
                    prev, nxt = flags(me + d2, p + (d1 if j else 0))
                    s3buf[c, j] = pick(c, j, prev, nxt)
                s3_copy(c).start()

        def cmp(cs):
            for c in cs:
                s3_copy(c).wait_recv()
            at = [pl.ds(pl.multiple_of(c * HD, HD), HD) for c in cs]
            chosen = []
            for c in cs:
                prev, nxt = flags(me, p + sides(c)[0])
                chosen.append(pick(c, 1, prev, nxt))
            each = range(len(cs))
            kh = [
                jnp.concatenate([kv[cs[u], 0, 0], chosen[u][0], kv[cs[u], 2, 0], kv[cs[u], 3, 0]], 0)
                for u in each
            ]
            vh = [
                jnp.concatenate([kv[cs[u], 0, 1], chosen[u][1], kv[cs[u], 2, 1], kv[cs[u], 3, 1]], 0)
                for u in each
            ]
            qh = [q[:, at[u]] for u in each]
            ga = [ga_all[:, at[u]] for u in each]
            scores = [lax.dot_general(qh[u], kh[u], NT, preferred_element_type=F32) for u in each]
            gp = [lax.dot_general(ga[u], vh[u], NT, preferred_element_type=F32) for u in each]
            scores = [scores[u] * (scale * LOG2E) + bias[cs[u] % 2] for u in each]
            e = [jnp.exp2(x - jnp.max(x, -1, keepdims=True)) for x in scores]
            probs = [x * (1.0 / jnp.sum(x, -1, keepdims=True)) for x in e]
            weights = [x.astype(BF16) for x in probs]
            attended = [
                jnp.dot(weights[u], vh[u], preferred_element_type=F32).astype(BF16) for u in each
            ]
            vt = [lax.dot_general(weights[u], ga[u], TN, preferred_element_type=F32) for u in each]
            delta = [
                jnp.sum(ga[u].astype(F32) * attended[u].astype(F32), -1, keepdims=True) for u in each
            ]
            gs = [(probs[u] * (gp[u] - delta[u])).astype(BF16) for u in each]
            kt = [
                lax.dot_general(gs[u], qh[u], TN, preferred_element_type=F32) * scale for u in each
            ]
            for u in each:
                for j in range(2):
                    r3send[cs[u], j, 0] = kt[u][(2 + j) * TILE:(3 + j) * TILE].astype(BF16)
                    r3send[cs[u], j, 1] = vt[u][(2 + j) * TILE:(3 + j) * TILE].astype(BF16)
            for c in cs:
                r3_copy(c).start()
            for u in each:
                qg = jnp.dot(gs[u], kh[u], preferred_element_type=F32) * scale
                qg_ref[:, at[u]] = qg.astype(BF16)
                att[:, at[u]] = attended[u]
                for j in range(2):
                    own[cs[u], j, 0] = kt[u][j * TILE:(j + 1) * TILE]
                    own[cs[u], j, 1] = vt[u][j * TILE:(j + 1) * TILE]

        def rz(cs):
            for c in cs:
                d1, d2 = sides(c)
                r3_copy(c).wait_recv()
                for j in range(2):
                    r = p + (d1 if j else 0)
                    mp, mn = flags(me, r)
                    op, on = flags(me + d2, r)
                    mp, mn, op, on = (x.astype(F32) for x in (mp, mn, op, on))
                    mine = own[c, j]
                    other = r3recv[c, j].astype(F32)
                    to_prev[c, j] = (mine * mp + other * op).astype(BF16)
                    to_next[c, j] = (mine * mn + other * on).astype(BF16)
                    own[c, j] = mine * (1.0 - mp - mn) + other * (1.0 - op - on)
                for out, copy, _ in zb_copies(c)[2:]:
                    pl.when(out)(copy.start)
            pl.when(k >= hold)(lambda: zb_own(cs))

        @pl.when(k == 0)
        def _():
            for kk in range(1, n_head):
                og_copy(kk).start()
            for n in range(lead):
                s1(pair(n))
                if n == 0:
                    for u in range(unit):
                        for out, copy, _ in z_copies(u)[:2]:
                            pl.when(out)(copy.start)
            set_bias()

        stage(-lead, s1)
        stage(AT_S2, s2)

        @pl.when(k == AT_S2)
        def _():
            for copy in local:
                copy.wait()
            for kk in range(1, n_head):
                og_arrival(kk).wait_recv()
            grads(0, blocks // 2)

        stage(AT_S3, s3)

        @pl.when(k == AT_S3)
        def _():
            grads(blocks // 2, blocks)

        @pl.when(k == hold)
        def _():
            each_pair(0, hold - AT_RZ, zb_own)

        @pl.when(k == steps + AT_CMP - 1)
        def _():
            each_pair(0, early, r1)

        stage(AT_CMP, cmp)

        @pl.when(k == steps + AT_CMP)
        def _():
            for kk in range(1, n_head):
                mix(kk)
            each_pair(early, steps - 2, r1)

        stage(AT_RZ, rz)
        return carry

    lead = min(LEAD, steps)
    block = 256 if cols % 256 == 0 else 128
    blocks = cols // block
    def grads(first, last):
        def one(n, carry):
            at = pl.ds(pl.multiple_of(n * block, 128), block)
            ga = lax.dot_general(og[...], w[at, :], NT, preferred_element_type=F32)
            ga_all[:, at] = ga.astype(BF16)
            return carry

        lax.fori_loop(first, last, one, 0)

    def m_copy(k):
        return rcopy(
            msend.at[k - 1], mrecv.at[k - 1], m_send.at[k - 1], m_recv.at[k - 1],
            {"head": (hd + k) % n_head},
        )

    def mix(k):
        base = ((hd + k) % n_head) * cols
        out = msend.at[k - 1] if k else mown

        def one(n, carry):
            src = pl.ds(pl.multiple_of(base + n * block, 128), block)
            dst = pl.ds(pl.multiple_of(n * block, 128), block)
            part = jnp.dot(att[...], w[:, src], preferred_element_type=F32)
            out[:, dst] = part.astype(BF16)
            return carry

        lax.fori_loop(0, blocks, one, 0)
        if k:
            m_copy(k).start()

    lax.fori_loop(0, steps + AT_RZ, step, 0)
    r1(pair(steps - 2))
    mix(0)
    r1(pair(steps - 1))
    for kk in range(1, n_head):
        m_copy(kk).wait_recv()
    total = mown[...].astype(F32)
    for kk in range(1, n_head):
        total = total + mrecv[kk - 1].astype(F32)
    mixed_ref[...] = total.astype(BF16)
    each_pair(0, steps, fin)

    def drain(c, carry):
        s1_copy(c).wait_send()
        s3_copy(c).wait_send()
        r3_copy(c).wait_send()
        r1_copy(c).wait_send()
        for out, copy, _ in z_copies(c) + zb_copies(c):
            pl.when(out)(copy.wait_send)
        return carry

    lax.fori_loop(0, heads, drain, 0)
    for k in range(1, n_head):
        og_copy(k).wait_send()
        m_copy(k).wait_send()


def hand_on(*refs):
    sems = refs[-1]
    n = len(refs) // 2
    copies = [pltpu.make_async_copy(refs[i], refs[n + i], sems.at[i]) for i in range(n)]
    for copy in copies:
        copy.start()
    for copy in copies:
        copy.wait()


def local(n_tm, n_head, queries, keys, values, out_weight, out_grad, align_lists, block_masks):
    rows, cols = queries.shape
    heads = cols // HD
    width = out_weight.shape[1]
    others = max(n_head - 1, 1)
    pair = (2, TILE, HD)
    hbm = pl.BlockSpec(memory_space=pltpu.HBM)
    vmem = pl.BlockSpec(memory_space=pltpu.VMEM)
    smem = pl.BlockSpec(memory_space=pltpu.SMEM)
    dma = pltpu.SemaphoreType.DMA
    V = pltpu.VMEM
    shapes = (
        jax.ShapeDtypeStruct((rows, cols), BF16),
        jax.ShapeDtypeStruct((rows, cols), BF16),
        jax.ShapeDtypeStruct(keys.shape, BF16),
        jax.ShapeDtypeStruct(keys.shape, BF16),
    )
    results = pl.pallas_call(
        functools.partial(kernel, n_tm, n_head, heads, rows),
        out_shape=tuple(V(x.shape, BF16) for x in shapes),
        in_specs=[smem, smem, hbm, hbm, hbm, hbm, hbm],
        out_specs=(vmem,) * 4,
        scratch_shapes=[
            V((rows, cols), BF16),
            V((cols, width), BF16),
            V((rows, width), BF16),
            V((rows, cols), BF16),
            V((rows, cols), BF16),
            V((2, rows, GROUP * TILE), F32),
            V((heads, 4) + pair, BF16),
            V((heads, 2) + pair, BF16),
            V((heads, 2) + pair, BF16),
            V((heads, 2) + pair, BF16),
            V((heads, 2) + pair, F32),
            V((heads, 2) + pair, BF16),
            V((heads, 2) + pair, BF16),
            V((heads, 2) + pair, BF16),
            V((heads, 2) + pair, BF16),
            V((heads, 2) + pair, BF16),
            V((heads, 2) + pair, BF16),
            V((heads,) + pair, BF16),
            V((heads,) + pair, BF16),
            V((others, rows, cols), BF16),
            V((others, rows, cols), BF16),
            V((rows, cols), BF16),
            dma((3,)),
            dma((heads, 2)),
            dma((others,)),
            dma((others,)),
            dma((others,)),
            dma((others,)),
            dma((heads,)),
            dma((heads,)),
            dma((heads, 4)),
            dma((heads, 4)),
            dma((heads,)),
            dma((heads,)),
            dma((heads,)),
            dma((heads,)),
            dma((heads, 4)),
            dma((heads, 4)),
            dma((heads,)),
            dma((heads,)),
        ],
        compiler_params=pltpu.CompilerParams(
            collective_id=0, has_side_effects=True, vmem_limit_bytes=59 * 1024 * 1024
        ),
        cost_estimate=pl.CostEstimate(
            flops=4 * rows * cols * width + 12 * rows * GROUP * TILE * cols,
            bytes_accessed=2 * cols * width, transcendentals=rows * GROUP * TILE * heads,
        ),
    )(align_lists.T, block_masks, queries, keys, values, out_weight, out_grad)
    return pl.pallas_call(
        hand_on,
        out_shape=shapes,
        in_specs=[vmem] * 4,
        out_specs=(pl.BlockSpec(memory_space=pltpu.HBM),) * 4,
        scratch_shapes=[dma((4,))],
        compiler_params=pltpu.CompilerParams(vmem_limit_bytes=1024 * 1024),
    )(*results)


def solution(mesh):
    split = P("tm", "head")
    return jax.shard_map(
        functools.partial(local, mesh.shape["tm"], mesh.shape["head"]),
        mesh=mesh,
        in_specs=(split, split, split, P("head", None), split, P(), P("tm", None)),
        out_specs=(split, split, split, split),
        check_vma=False,
    )
```

```python
import functools
import math

import jax
import jax.numpy as jnp
from jax import lax
from jax.experimental import pallas as pl
from jax.experimental.pallas import tpu as pltpu
from jax.sharding import PartitionSpec as P

HD = 128
TILE = 128
GROUP = 4
LIST = 4
BLOCKS = 3
MESH = pl.DeviceIdType.MESH
NT = (((1,), (1,)), ((), ()))
TN = (((0,), (0,)), ((), ()))
LEAD = 5
AT_S2, AT_S3, AT_CMP, AT_RZ = 1, 2, 3, 4
F32 = jnp.float32
LOG2E = math.log2(math.e)
BF16 = jnp.bfloat16


def kernel(
    n_tm, n_head, heads, rows,
    align, masks, q_hbm, k_hbm, v_hbm, w_hbm, og_hbm,
    mixed_ref, qg_ref, kg_ref, vg_ref,
    q, w, og, ga_all, att, bias,
    kv, zprev, znext, s3buf,
    own, r3send, r3recv, to_prev, to_next, of_next, of_prev, r1send, r1recv,
    msend, mrecv, mown,
    loc_sem, kv_sem, og_send, og_recv, m_send, m_recv,
    s1_send, s1_recv, z_send, z_recv, s3_send, s3_recv,
    r3_ssem, r3_rsem, zb_send, zb_recv, r1_ssem, r1_rsem,
):
    scale = 1.0 / math.sqrt(HD)
    me = lax.axis_index("tm")
    hd = lax.axis_index("head")
    cols = heads * HD
    planes = n_tm // GROUP
    plane = me // GROUP
    p = me % GROUP
    dx = 1 - 2 * (p % 2)
    dy = 2 - 4 * (p // 2)
    has_prev = plane > 0
    has_next = plane < planes - 1

    unit = 2 if heads % 2 == 0 else 1
    steps = heads // unit

    def sides(c):
        t = c % 2
        d1 = dx * (1 - t) + dy * t
        d2 = dy * (1 - t) + dx * t
        return d1, d2

    def flags(dest, r):
        prev = jnp.int32(0)
        nxt = jnp.int32(0)
        for s in range(LIST):
            a = align[s, dest]
            hit = jnp.logical_and(a >= 0, lax.rem(a + GROUP, GROUP) == r)
            pa = lax.div(a + GROUP, GROUP) - 1
            prev = jnp.where(jnp.logical_and(hit, pa < plane), 1, prev)
            nxt = jnp.where(jnp.logical_and(hit, pa > plane), 1, nxt)
        return prev, nxt

    def rcopy(src, dst, ss, rs, dev):
        return pltpu.make_async_remote_copy(
            src_ref=src, dst_ref=dst, send_sem=ss, recv_sem=rs,
            device_id=dev, device_id_type=MESH,
        )

    def s1_copy(c):
        d1, _ = sides(c)
        return rcopy(kv.at[c, 0], kv.at[c, 1], s1_send.at[c], s1_recv.at[c], {"tm": me + d1})

    def s3_copy(c):
        _, d2 = sides(c)
        return rcopy(
            s3buf.at[c], kv.at[c, pl.ds(2, 2)], s3_send.at[c], s3_recv.at[c], {"tm": me + d2}
        )

    def r3_copy(c):
        _, d2 = sides(c)
        return rcopy(r3send.at[c], r3recv.at[c], r3_ssem.at[c], r3_rsem.at[c], {"tm": me + d2})

    def r1_copy(c):
        d1, _ = sides(c)
        return rcopy(r1send.at[c], r1recv.at[c], r1_ssem.at[c], r1_rsem.at[c], {"tm": me + d1})

    def z_copies(c):
        d1, d2 = sides(c)
        out = []
        for j in range(2):
            r = p + (d1 if j else 0)
            up = jnp.logical_or(r > p, r > p + d2)
            down = jnp.logical_or(r < p, r < p + d2)
            out.append((
                jnp.logical_and(up, has_next),
                rcopy(kv.at[c, j], zprev.at[c, j], z_send.at[c, j], z_recv.at[c, j],
                      {"tm": me + GROUP}),
                jnp.logical_and(up, has_prev),
            ))
            out.append((
                jnp.logical_and(down, has_prev),
                rcopy(kv.at[c, j], znext.at[c, j], z_send.at[c, 2 + j], z_recv.at[c, 2 + j],
                      {"tm": me - GROUP}),
                jnp.logical_and(down, has_next),
            ))
        return out

    def zb_copies(c):
        d1, d2 = sides(c)
        out = []
        for j in range(2):
            r = p + (d1 if j else 0)
            up = jnp.logical_or(r > p, r > p + d2)
            down = jnp.logical_or(r < p, r < p + d2)
            out.append((
                jnp.logical_and(up, has_prev),
                rcopy(to_prev.at[c, j], of_next.at[c, j], zb_send.at[c, j], zb_recv.at[c, j],
                      {"tm": me - GROUP}),
                jnp.logical_and(up, has_next),
            ))
            out.append((
                jnp.logical_and(down, has_next),
                rcopy(to_next.at[c, j], of_prev.at[c, j], zb_send.at[c, 2 + j],
                      zb_recv.at[c, 2 + j], {"tm": me + GROUP}),
                jnp.logical_and(down, has_prev),
            ))
        return out

    def kv_copies(c):
        at = pl.ds(pl.multiple_of(c * HD, HD), HD)
        return (
            pltpu.make_async_copy(k_hbm.at[:, at], kv.at[c, 0, 0], kv_sem.at[c, 0]),
            pltpu.make_async_copy(v_hbm.at[:, at], kv.at[c, 0, 1], kv_sem.at[c, 1]),
        )

    def start_kv(c, carry):
        for copy in kv_copies(c):
            copy.start()
        return carry

    lax.fori_loop(0, heads, start_kv, 0)

    og_own = pl.ds(pl.multiple_of(hd * cols, HD), cols)
    local = (
        pltpu.make_async_copy(og_hbm, og.at[:, og_own], loc_sem.at[0]),
        pltpu.make_async_copy(q_hbm, q, loc_sem.at[1]),
        pltpu.make_async_copy(w_hbm, w, loc_sem.at[2]),
    )
    for copy in local:
        copy.start()

    barrier = pltpu.get_barrier_semaphore()
    pl.semaphore_signal(barrier, inc=1, device_id={"tm": me + dx}, device_id_type=MESH)
    pl.semaphore_signal(barrier, inc=1, device_id={"tm": me + dy}, device_id_type=MESH)

    @pl.when(has_prev)
    def _():
        pl.semaphore_signal(barrier, inc=1, device_id={"tm": me - GROUP}, device_id_type=MESH)

    @pl.when(has_next)
    def _():
        pl.semaphore_signal(barrier, inc=1, device_id={"tm": me + GROUP}, device_id_type=MESH)

    for k in range(1, n_head):
        pl.semaphore_signal(
            barrier, inc=1, device_id={"head": (hd + k) % n_head}, device_id_type=MESH
        )

    near = 2 + (n_head - 1) + jnp.where(has_prev, 1, 0) + jnp.where(has_next, 1, 0)
    pl.semaphore_wait(barrier, near)

    def set_bias():
        row = lax.broadcasted_iota(jnp.int32, (rows, GROUP * TILE), 0)
        col = lax.broadcasted_iota(jnp.int32, (rows, GROUP * TILE), 1)
        for t in range(2):
            d1, d2 = sides(t)
            residues = (p, p + d1, p + d2, p + d1 + d2)
            total = jnp.full((rows, GROUP * TILE), -1e30, F32)
            for i in range(rows // TILE):
                for j, r in enumerate(residues):
                    live = jnp.float32(-1e30)
                    for b in range(BLOCKS):
                        m = masks[i, b]
                        for s in range(LIST):
                            a = align[s, me]
                            hit = jnp.logical_and(m == s, lax.rem(a + GROUP, GROUP) == r)
                            live = jnp.where(hit, jnp.float32(0.0), live)
                    here = jnp.logical_and(row // TILE == i, col // TILE == j)
                    total = jnp.where(here, live, total)
            bias[t] = total

    def og_copy(k):
        return rcopy(
            og_hbm, og.at[:, og_own], og_send.at[k - 1], og_recv.at[k - 1],
            {"head": (hd + k) % n_head},
        )

    def og_arrival(k):
        src = (hd - k + n_head) % n_head
        return rcopy(
            og_hbm, og.at[:, pl.ds(pl.multiple_of(src * cols, HD), cols)],
            og_send.at[k - 1], og_recv.at[k - 1], {"head": (hd + k) % n_head},
        )

    def pick(c, j, prev, nxt):
        return jnp.where(prev > 0, zprev[c, j], jnp.where(nxt > 0, znext[c, j], kv[c, j]))

    def back(c, j):
        copies = zb_copies(c)[2 * j:2 * j + 2]
        for _, copy, come in copies:
            pl.when(come)(copy.wait_recv)
        total = own[c, j]
        total = total + jnp.where(copies[0][2], of_next[c, j].astype(F32), 0.0)
        return total + jnp.where(copies[1][2], of_prev[c, j].astype(F32), 0.0)

    def r1(cs):
        for c in cs:
            r1send[c] = back(c, 1).astype(BF16)
            r1_copy(c).start()

    def fin(cs):
        for c in cs:
            total = back(c, 0)
            r1_copy(c).wait_recv()
            at = pl.ds(pl.multiple_of(c * HD, HD), HD)
            kg_ref[:, at] = (total[0] + r1recv[c, 0].astype(F32)).astype(BF16)
            vg_ref[:, at] = (total[1] + r1recv[c, 1].astype(F32)).astype(BF16)

    def pair(n):
        return [n * unit + u for u in range(unit)]

    def each_pair(first, last, body):
        def one(n, carry):
            body(pair(n))
            return carry

        lax.fori_loop(first, last, one, 0)

    def step(k, carry):
        def stage(skew, body):
            n = k - skew
            pl.when(jnp.logical_and(n >= 0, n < steps))(lambda: body(pair(n)))

        def s1(cs):
            for c in cs:
                for copy in kv_copies(c):
                    copy.wait()
                s1_copy(c).start()

        def s2(cs):
            for c in cs:
                s1_copy(c).wait_recv()
                mine, theirs = z_copies(c)[:2], z_copies(c)[2:]
                for out, copy, _ in mine:
                    pl.when(jnp.logical_and(out, k > AT_S2))(copy.start)
                for out, copy, _ in theirs:
                    pl.when(out)(copy.start)

        def s3(cs):
            for c in cs:
                for _, copy, come in z_copies(c):
                    pl.when(come)(copy.wait_recv)
                d1, d2 = sides(c)
                for j in range(2):
                    prev, nxt = flags(me + d2, p + (d1 if j else 0))
                    s3buf[c, j] = pick(c, j, prev, nxt)
                s3_copy(c).start()

        def cmp(cs):
            for c in cs:
                s3_copy(c).wait_recv()
            at = [pl.ds(pl.multiple_of(c * HD, HD), HD) for c in cs]
            chosen = []
            for c in cs:
                prev, nxt = flags(me, p + sides(c)[0])
                chosen.append(pick(c, 1, prev, nxt))
            each = range(len(cs))
            kh = [
                jnp.concatenate([kv[cs[u], 0, 0], chosen[u][0], kv[cs[u], 2, 0], kv[cs[u], 3, 0]], 0)
                for u in each
            ]
            vh = [
                jnp.concatenate([kv[cs[u], 0, 1], chosen[u][1], kv[cs[u], 2, 1], kv[cs[u], 3, 1]], 0)
                for u in each
            ]
            qh = [q[:, at[u]] for u in each]
            ga = [ga_all[:, at[u]] for u in each]
            scores = [lax.dot_general(qh[u], kh[u], NT, preferred_element_type=F32) for u in each]
            gp = [lax.dot_general(ga[u], vh[u], NT, preferred_element_type=F32) for u in each]
            scores = [scores[u] * (scale * LOG2E) + bias[cs[u] % 2] for u in each]
            e = [jnp.exp2(x - jnp.max(x, -1, keepdims=True)) for x in scores]
            probs = [x * (1.0 / jnp.sum(x, -1, keepdims=True)) for x in e]
            weights = [x.astype(BF16) for x in probs]
            attended = [
                jnp.dot(weights[u], vh[u], preferred_element_type=F32).astype(BF16) for u in each
            ]
            vt = [lax.dot_general(weights[u], ga[u], TN, preferred_element_type=F32) for u in each]
            delta = [
                jnp.sum(ga[u].astype(F32) * attended[u].astype(F32), -1, keepdims=True) for u in each
            ]
            gs = [(probs[u] * (gp[u] - delta[u])).astype(BF16) for u in each]
            kt = [
                lax.dot_general(gs[u], qh[u], TN, preferred_element_type=F32) * scale for u in each
            ]
            for u in each:
                for j in range(2):
                    r3send[cs[u], j, 0] = kt[u][(2 + j) * TILE:(3 + j) * TILE].astype(BF16)
                    r3send[cs[u], j, 1] = vt[u][(2 + j) * TILE:(3 + j) * TILE].astype(BF16)
            for c in cs:
                r3_copy(c).start()
            for u in each:
                qg = jnp.dot(gs[u], kh[u], preferred_element_type=F32) * scale
                qg_ref[:, at[u]] = qg.astype(BF16)
                att[:, at[u]] = attended[u]
                for j in range(2):
                    own[cs[u], j, 0] = kt[u][j * TILE:(j + 1) * TILE]
                    own[cs[u], j, 1] = vt[u][j * TILE:(j + 1) * TILE]

        def rz(cs):
            for c in cs:
                r3_copy(c).wait_recv()
            for j in (1, 0):
                for c in cs:
                    split(c, j)

        def split(c, j):
            d1, d2 = sides(c)
            r = p + (d1 if j else 0)
            mp, mn = flags(me, r)
            op, on = flags(me + d2, r)
            mp, mn, op, on = (x.astype(F32) for x in (mp, mn, op, on))
            (prev_out, prev_copy, _), (next_out, next_copy, _) = zb_copies(c)[2 * j:2 * j + 2]

            @pl.when(prev_out)
            def _():
                to_prev[c, j] = (own[c, j] * mp + r3recv[c, j].astype(F32) * op).astype(BF16)
                prev_copy.start()

            @pl.when(next_out)
            def _():
                to_next[c, j] = (own[c, j] * mn + r3recv[c, j].astype(F32) * on).astype(BF16)
                next_copy.start()

            own[c, j] = (
                own[c, j] * (1.0 - mp - mn) + r3recv[c, j].astype(F32) * (1.0 - op - on)
            )

        @pl.when(k == 0)
        def _():
            for kk in range(1, n_head):
                og_copy(kk).start()
            for n in range(lead):
                s1(pair(n))
                if n == 0:
                    for u in range(unit):
                        for out, copy, _ in z_copies(u)[:2]:
                            pl.when(out)(copy.start)
            set_bias()

        stage(-lead, s1)
        stage(AT_S2, s2)

        @pl.when(k == AT_S2)
        def _():
            for copy in local:
                copy.wait()
            for kk in range(1, n_head):
                og_arrival(kk).wait_recv()
            grads(0, blocks // 2)

        stage(AT_S3, s3)

        @pl.when(k == AT_S3)
        def _():
            grads(blocks // 2, blocks)

        stage(AT_CMP, cmp)

        @pl.when(k == steps + AT_CMP)
        def _():
            for kk in range(1, n_head):
                mix(kk)
            each_pair(0, steps - 2, r1)

        stage(AT_RZ, rz)
        return carry

    lead = min(LEAD, steps)
    block = 256 if cols % 256 == 0 else 128
    blocks = cols // block
    def grads(first, last):
        def one(n, carry):
            at = pl.ds(pl.multiple_of(n * block, 128), block)
            ga = lax.dot_general(og[...], w[at, :], NT, preferred_element_type=F32)
            ga_all[:, at] = ga.astype(BF16)
            return carry

        lax.fori_loop(first, last, one, 0)

    def m_copy(k):
        return rcopy(
            msend.at[k - 1], mrecv.at[k - 1], m_send.at[k - 1], m_recv.at[k - 1],
            {"head": (hd + k) % n_head},
        )

    def mix(k):
        base = ((hd + k) % n_head) * cols
        out = msend.at[k - 1] if k else mown

        def one(n, carry):
            src = pl.ds(pl.multiple_of(base + n * block, 128), block)
            dst = pl.ds(pl.multiple_of(n * block, 128), block)
            part = jnp.dot(att[...], w[:, src], preferred_element_type=F32)
            out[:, dst] = part.astype(BF16)
            return carry

        lax.fori_loop(0, blocks, one, 0)
        if k:
            m_copy(k).start()

    lax.fori_loop(0, steps + AT_RZ, step, 0)
    r1(pair(steps - 2))
    mix(0)
    r1(pair(steps - 1))
    for kk in range(1, n_head):
        m_copy(kk).wait_recv()
    total = mown[...].astype(F32)
    for kk in range(1, n_head):
        total = total + mrecv[kk - 1].astype(F32)
    mixed_ref[...] = total.astype(BF16)
    each_pair(0, steps, fin)

    def drain(c, carry):
        s1_copy(c).wait_send()
        s3_copy(c).wait_send()
        r3_copy(c).wait_send()
        r1_copy(c).wait_send()
        for out, copy, _ in z_copies(c) + zb_copies(c):
            pl.when(out)(copy.wait_send)
        return carry

    lax.fori_loop(0, heads, drain, 0)
    for k in range(1, n_head):
        og_copy(k).wait_send()
        m_copy(k).wait_send()


def hand_on(*refs):
    sems = refs[-1]
    n = len(refs) // 2
    copies = [pltpu.make_async_copy(refs[i], refs[n + i], sems.at[i]) for i in range(n)]
    for copy in copies:
        copy.start()
    for copy in copies:
        copy.wait()


def local(n_tm, n_head, queries, keys, values, out_weight, out_grad, align_lists, block_masks):
    rows, cols = queries.shape
    heads = cols // HD
    width = out_weight.shape[1]
    others = max(n_head - 1, 1)
    pair = (2, TILE, HD)
    hbm = pl.BlockSpec(memory_space=pltpu.HBM)
    vmem = pl.BlockSpec(memory_space=pltpu.VMEM)
    smem = pl.BlockSpec(memory_space=pltpu.SMEM)
    dma = pltpu.SemaphoreType.DMA
    V = pltpu.VMEM
    shapes = (
        jax.ShapeDtypeStruct((rows, cols), BF16),
        jax.ShapeDtypeStruct((rows, cols), BF16),
        jax.ShapeDtypeStruct(keys.shape, BF16),
        jax.ShapeDtypeStruct(keys.shape, BF16),
    )
    results = pl.pallas_call(
        functools.partial(kernel, n_tm, n_head, heads, rows),
        out_shape=tuple(V(x.shape, BF16) for x in shapes),
        in_specs=[smem, smem, hbm, hbm, hbm, hbm, hbm],
        out_specs=(vmem,) * 4,
        scratch_shapes=[
            V((rows, cols), BF16),
            V((cols, width), BF16),
            V((rows, width), BF16),
            V((rows, cols), BF16),
            V((rows, cols), BF16),
            V((2, rows, GROUP * TILE), F32),
            V((heads, 4) + pair, BF16),
            V((heads, 2) + pair, BF16),
            V((heads, 2) + pair, BF16),
            V((heads, 2) + pair, BF16),
            V((heads, 2) + pair, F32),
            V((heads, 2) + pair, BF16),
            V((heads, 2) + pair, BF16),
            V((heads, 2) + pair, BF16),
            V((heads, 2) + pair, BF16),
            V((heads, 2) + pair, BF16),
            V((heads, 2) + pair, BF16),
            V((heads,) + pair, BF16),
            V((heads,) + pair, BF16),
            V((others, rows, cols), BF16),
            V((others, rows, cols), BF16),
            V((rows, cols), BF16),
            dma((3,)),
            dma((heads, 2)),
            dma((others,)),
            dma((others,)),
            dma((others,)),
            dma((others,)),
            dma((heads,)),
            dma((heads,)),
            dma((heads, 4)),
            dma((heads, 4)),
            dma((heads,)),
            dma((heads,)),
            dma((heads,)),
            dma((heads,)),
            dma((heads, 4)),
            dma((heads, 4)),
            dma((heads,)),
            dma((heads,)),
        ],
        compiler_params=pltpu.CompilerParams(
            collective_id=0, has_side_effects=True, vmem_limit_bytes=59 * 1024 * 1024
        ),
        cost_estimate=pl.CostEstimate(
            flops=4 * rows * cols * width + 12 * rows * GROUP * TILE * cols,
            bytes_accessed=2 * cols * width, transcendentals=rows * GROUP * TILE * heads,
        ),
    )(align_lists.T, block_masks, queries, keys, values, out_weight, out_grad)
    return pl.pallas_call(
        hand_on,
        out_shape=shapes,
        in_specs=[vmem] * 4,
        out_specs=(pl.BlockSpec(memory_space=pltpu.HBM),) * 4,
        scratch_shapes=[dma((4,))],
        compiler_params=pltpu.CompilerParams(vmem_limit_bytes=1024 * 1024),
    )(*results)


def solution(mesh):
    split = P("tm", "head")
    return jax.shard_map(
        functools.partial(local, mesh.shape["tm"], mesh.shape["head"]),
        mesh=mesh,
        in_specs=(split, split, split, P("head", None), split, P(), P("tm", None)),
        out_specs=(split, split, split, split),
        check_vma=False,
    )
```
